32 devices in a mesh: leaf: 8 (over z, y), grp: 4 (over x, core).
Axes of the slice: x: 2, y: 2, z: 4, core: 2. Of those that a mesh axis runs over, the one named last changes fastest.
Arguments:
- vectors: bfloat16 [32, 65536], P(None, ('leaf', 'grp')), may hold values from -6 to 6
- leaf_basis: bfloat16 [256, 64, 256], P(('leaf', 'grp')), may hold values from -0.375 to 0.375
- transfer: float32 [2, 64, 64], replicated, may hold values from -0.625 to 0.625
- sibling_coupling: float32 [2, 64, 64], replicated, may hold values from -0.75 to 0.75
- list_coupling: float32 [8, 64, 64], replicated, may hold values from -0.4375 to 0.4375
- near_tiles: bfloat16 [512, 256, 256], P(('leaf', 'grp')), may hold values from -0.375 to 0.375
- tile_target: int32 [512], P(('leaf', 'grp')), may hold values from 0 to 7
- tile_source: int32 [512], P(('leaf', 'grp')), may hold values from 0 to 23, as said below
- tile_count: int32 [32], P(('leaf', 'grp')), may hold values from 8 to 16, as said below
- couple_offset: int32 [32, 3], P(('leaf', 'grp')), may hold values from -2 to 2, as said below
- couple_class: int32 [32, 3], P(('leaf', 'grp')), may hold values from 0 to 7
Outputs:
- field: float32 [32, 65536], P(None, ('leaf', 'grp'))
The draws below stay inside these ranges and needn't reach their ends.
Inputs may be any that keep to these rules, and one draw needn't show every extreme that they name: Only a device's first tile_count slots hold live tiles; some device uses all 16 slots. `tile_source`: over all 16 slots of a device, live or not, the sources in the window's first 8 boxes name at most 4 distinct boxes, and so do those in its last 8 boxes; on every device the live tiles name 4 boxes on both sides. `couple_offset`: never zero.
All inputs are finite; a program needn't handle non-finite values.
Results may differ from the reference program's by a relative error of at most 0.0024.
Values may be sent and summed in bfloat16 or wider, within the bound.
No kernel may reach another device: no remote copies, remote signals or barrier semaphores. Data moves between devices by JAX's collectives and lax.ppermute only.
A program may use at most 64 MiB of HBM per device.

```python
import jax
import jax.numpy as jnp
from jax import lax

POINTS = 256
VECTORS = 32
RANK = 64
BOXES = 8
SLOTS = 16
LINKS = 3
REACH = 2
CLASSES = 8
NBOX = 256
NPTS = 65536
NTILE = 512
N_LEAF = 8
N_GRP = 4


def draw_tile_count(key, part):
    key = jax.random.fold_in(key, 11)
    first_key, second_key = jax.random.split(key)
    devices = N_LEAF * N_GRP
    shifts = jax.random.randint(first_key, (devices,), 0, 5)
    counts = jnp.right_shift(jnp.full((devices,), SLOTS, jnp.int32), shifts.astype(jnp.int32))
    counts = jnp.maximum(counts, BOXES)
    busiest = jax.random.randint(second_key, (), 0, devices)
    counts = jnp.where(jnp.arange(devices, dtype=jnp.int32) == busiest, SLOTS, counts)
    return counts.astype(jnp.int32)


def draw_tile_source(key, part):
    key = jax.random.fold_in(key, 37)
    devices = N_LEAF * N_GRP
    half_boxes = BOXES // 2
    left_key, right_key, role_key = jax.random.split(key, 3)
    left_sets = jax.vmap(lambda one_key: jax.random.permutation(one_key, BOXES))(jax.random.split(left_key, devices))[:, :half_boxes]
    right_sets = jax.vmap(lambda one_key: jax.random.permutation(one_key, BOXES))(jax.random.split(right_key, devices))[:, :half_boxes]
    own_boxes = jnp.broadcast_to(BOXES + jnp.arange(BOXES, dtype=jnp.int32)[None, :], (devices, BOXES))
    candidates = jnp.concatenate([left_sets.astype(jnp.int32), own_boxes.astype(jnp.int32), 2 * BOXES + right_sets.astype(jnp.int32)], axis=1)
    free_roles = jax.random.randint(role_key, (devices, SLOTS), 0, 2 * half_boxes + BOXES).astype(jnp.int32)
    slot_ids = jnp.broadcast_to(jnp.arange(SLOTS, dtype=jnp.int32)[None, :], (devices, SLOTS))
    forced = jnp.where(slot_ids % 2 == 0, slot_ids // 2, half_boxes + BOXES + slot_ids // 2)
    roles = jnp.where(slot_ids < BOXES, forced, free_roles).astype(jnp.int32)
    sources = jnp.take_along_axis(candidates, roles, axis=1)
    return sources.reshape(devices * SLOTS).astype(jnp.int32)


def draw_couple_offset(key, part):
    key = jax.random.fold_in(key, 23)
    first_key, second_key = jax.random.split(key)
    devices = N_LEAF * N_GRP
    magnitude = jax.random.randint(first_key, (devices, LINKS), 1, REACH + 1)
    signs = jax.random.randint(second_key, (devices, LINKS), 0, 2) * 2 - 1
    offsets = magnitude * signs
    offsets = offsets.at[0, 0].set(0 - REACH)
    offsets = offsets.at[0, 1].set(REACH)
    return offsets.astype(jnp.int32)


def plant(drawn, key, smallest, high):
    longest = drawn.shape.index(max(drawn.shape))
    spots = []
    for shift in (0, 1):
        where = [jax.random.randint(jax.random.fold_in(key, axis), (), 0, length) for axis, length in enumerate(drawn.shape)]
        where[longest] = (where[longest] + shift) % drawn.shape[longest]
        spots.append(tuple(where))
    return drawn.at[spots[0]].set(smallest).at[spots[1]].set(high)


def steps_of(stream_key, dims, pieces, low, top_value):
    def one(dim, shards_of):
        heights = jax.random.uniform(jax.random.fold_in(jax.random.fold_in(stream_key, 6), dim), (shards_of,), jnp.float32, low / len(pieces), top_value / len(pieces))
        return jnp.repeat(jnp.exp(heights), dims[dim] // shards_of).reshape((-1,) + (1,) * (len(dims) - dim - 1))

    level = one(*pieces[0])
    for cut in pieces[1:]:
        level = level * one(*cut)
    return level


def bell_draw(rng, dims, width, reach, shards=(), kind=jnp.bfloat16):
    factor_of = steps_of(rng, dims, shards, -0.22, 0.18) if shards else 1.0
    result = jax.random.normal(rng, dims, jnp.float32) * width * factor_of
    return jnp.minimum(jnp.maximum(result, -reach), reach).astype(kind)


def setup_inputs(seed: int = 0) -> dict:
    streams_of = jax.random.split(jax.random.key(seed), 12)
    return {
        "vectors": bell_draw(streams_of[0], (VECTORS, NPTS), 1.0, 6.0, ((1, 32),)),
        "leaf_basis": bell_draw(streams_of[1], (NBOX, RANK, POINTS), POINTS ** -0.5, 0.375, ((0, 32),)),
        "transfer": bell_draw(streams_of[2], (2, RANK, RANK), (RANK * 17 // 12) ** -0.5, 0.625, (), jnp.float32),
        "sibling_coupling": bell_draw(streams_of[3], (2, RANK, RANK), RANK ** -0.5, 0.75, (), jnp.float32),
        "list_coupling": bell_draw(streams_of[4], (CLASSES, RANK, RANK), (RANK * LINKS) ** -0.5, 0.4375, (), jnp.float32),
        "near_tiles": bell_draw(streams_of[5], (NTILE, POINTS, POINTS), POINTS ** -0.5, 0.375, ((0, 32),)),
        "tile_target": plant(jax.random.randint(streams_of[6], (NTILE,), 0, BOXES), jax.random.fold_in(streams_of[6], 1), 0, BOXES - 1).astype(jnp.int32),
        "tile_source": draw_tile_source(jax.random.fold_in(streams_of[11], 71), 0),
        "tile_count": draw_tile_count(jax.random.fold_in(streams_of[11], 71), 0),
        "couple_offset": draw_couple_offset(jax.random.fold_in(streams_of[11], 71), 0),
        "couple_class": plant(jax.random.randint(streams_of[10], (N_LEAF * N_GRP, LINKS), 0, CLASSES), jax.random.fold_in(streams_of[10], 1), 0, CLASSES - 1).astype(jnp.int32),
    }


HIGH = lax.Precision.HIGHEST


def pair_up(coeffs, transfer):
    halves = coeffs.shape[0] // 2
    paired = coeffs.reshape(halves, 2, coeffs.shape[1], coeffs.shape[2])
    return jnp.einsum("nsrk,skj->nrj", paired, transfer, precision=HIGH)


def descend(local_exp, coeffs, transfer, sibling_coupling):
    halves = coeffs.shape[0] // 2
    paired = coeffs.reshape(halves, 2, coeffs.shape[1], coeffs.shape[2])
    downward = jnp.einsum("prj,skj->psrk", local_exp, transfer, precision=HIGH)
    across = jnp.einsum("psrk,skj->psrj", paired[:, ::-1], sibling_coupling, precision=HIGH)
    return (downward + across).reshape(coeffs.shape)


def reference(vectors, leaf_basis, transfer, sibling_coupling, list_coupling, near_tiles, tile_target, tile_source, tile_count, couple_offset, couple_class):
    box_total = leaf_basis.shape[0]
    devices = tile_count.shape[0]
    boxes_here = box_total // devices
    blocks = vectors.reshape(VECTORS, box_total, POINTS).transpose(1, 0, 2)
    leaf = jnp.einsum("bkp,brp->brk", leaf_basis.astype(jnp.float32), blocks.astype(jnp.float32), precision=HIGH)
    levels = [leaf]
    while levels[-1].shape[0] > 1:
        levels.append(pair_up(levels[-1], transfer))
    device_level = boxes_here.bit_length() - 1
    local_exp = jnp.zeros((1, VECTORS, RANK), jnp.float32)
    for depth_level in range(len(levels) - 2, -1, -1):
        local_exp = descend(local_exp, levels[depth_level], transfer, sibling_coupling)
        if depth_level == device_level:
            partners = (jnp.arange(devices, dtype=jnp.int32)[:, None] + couple_offset) % devices
            linked = levels[depth_level][partners]
            matrices = list_coupling[couple_class]
            local_exp = local_exp + jnp.einsum("dcrk,dckj->drj", linked, matrices, precision=HIGH)
    rounded = lax.optimization_barrier(local_exp.astype(jnp.bfloat16)).astype(jnp.float32)
    far_field = jnp.einsum("brk,bkp->brp", rounded, leaf_basis.astype(jnp.float32), precision=HIGH)
    tile_set = near_tiles.reshape(devices, SLOTS, POINTS, POINTS)
    targets = tile_target.reshape(devices, SLOTS)
    sources = tile_source.reshape(devices, SLOTS)

    def one_device(record):
        device, tiles_here, target_here, source_here, count_here = record
        chosen = (device * boxes_here - boxes_here + source_here) % box_total
        inputs = blocks[chosen].astype(jnp.float32)
        products = jnp.einsum("trp,tpq->trq", inputs, tiles_here.astype(jnp.float32), precision=HIGH)
        live = (jnp.arange(SLOTS, dtype=jnp.int32) < count_here).astype(jnp.float32)
        placing = (target_here[:, None] == jnp.arange(boxes_here, dtype=jnp.int32)[None, :]).astype(jnp.float32) * live[:, None]
        return jnp.einsum("tb,trq->brq", placing, products, precision=HIGH)

    near_field = lax.map(one_device, (jnp.arange(devices, dtype=jnp.int32), tile_set, targets, sources, tile_count))
    field = near_field.reshape(box_total, VECTORS, POINTS) + far_field
    return field.transpose(1, 0, 2).reshape(VECTORS, box_total * POINTS)
```

```python
import functools

import jax
import jax.numpy as jnp
from jax import lax
from jax.experimental import pallas as pl
from jax.experimental.pallas import tpu as pltpu
from jax.sharding import PartitionSpec as P

AXES = ("leaf", "grp")
F32 = jnp.float32
BF16 = jnp.bfloat16
NN = (((1,), (0,)), ((), ()))
NT = (((1,), (1,)), ((), ()))
CHUNK = 512
VMEM_LIMIT = 48 * 2**20


def split(x):
    high = x.astype(BF16)
    return high, (x - high.astype(F32)).astype(BF16)


def dot(a, b, dims=NN):
    return lax.dot_general(a, b, dims, preferred_element_type=F32)


def dot3(a, b, dims=NN):
    a_high, a_low = split(a)
    b_high, b_low = split(b)
    return dot(a_high, b_high, dims) + (dot(a_low, b_high, dims) + dot(a_high, b_low, dims))


def rounds_of(bits):
    rounds = []
    top = bits
    while top > 0:
        wide = 2 if top > 1 else 1
        rounds.append((top - wide, wide))
        top -= wide
    return rounds


def masks_of(bits):
    masks = [0]
    for low, wide in rounds_of(bits):
        masks = [mask ^ (step << low) for step in range(2**wide) for mask in masks]
    return masks


def place_of(mask, bits):
    place, shift = 0, 0
    for low, wide in rounds_of(bits):
        place = place | (((mask >> low) & (2**wide - 1)) << shift)
        shift += wide
    return place


def up(blocks, transfer):
    left = jnp.concatenate(blocks[0::2], axis=0)
    right = jnp.concatenate(blocks[1::2], axis=0)
    rows = blocks[0].shape[0]
    total = dot3(left, transfer[0]) + dot3(right, transfer[1])
    return [total[i * rows : (i + 1) * rows] for i in range(len(blocks) // 2)]


def leaf_kernel(vectors, basis, transfer, send, leaf):
    boxes, _, points = basis.shape
    level = []
    for b in range(boxes):
        level.append(dot(vectors[:, b * points : (b + 1) * points], basis[b], NT))
        leaf[b] = level[b]
    pair = (transfer[0], transfer[1])
    while len(level) > 1:
        level = up(level, pair)
    send[0] = jnp.concatenate(split(level[0]), axis=1)


def map_kernel(bits, device, offsets, classes, leaf, transfer, sibling, coupling, maps, spread, local, stack):
    boxes, columns, rank = leaf.shape
    me = device[0]
    count = 2**bits
    places = {mask: k for k, mask in enumerate(masks_of(bits))}
    t0, t1 = transfer[0], transfer[1]
    s0, s1 = sibling[0], sibling[1]

    def put(at, block):
        both = jnp.concatenate(split(block), axis=1)
        maps[pl.ds(at, rank)] = both
        maps[pl.ds(at + rank, rank)] = both

    put(0, jnp.zeros((rank, rank), F32))
    for height in range(bits):
        mine = (me >> height) & 1
        rows = 2**height * rank
        if height == 0:
            put(places[1] * 2 * rank, sibling[mine])
            stack[0:rank] = transfer[mine]
            stack[rank : 2 * rank] = transfer[1 - mine]
            continue
        bridge = dot3(sibling[mine], stack[0:rank], NT)
        near, far = transfer[mine], transfer[1 - mine]
        for start in range(0, rows, CHUNK):
            size = min(CHUNK, rows - start)
            part = stack[start : start + size]
            block = dot3(part, bridge)
            for i in range(size // rank):
                at = places[2**height + start // rank + i] * 2 * rank
                put(at, block[i * rank : (i + 1) * rank])
            if height + 1 < bits:
                stack[rows + start : rows + start + size] = dot3(part, far)
                stack[start : start + size] = dot3(part, near)
    for i in range(offsets.shape[1]):
        mask = ((me + offsets[0, i] + count) & (count - 1)) ^ me
        at = pl.multiple_of(place_of(mask, bits) * 2 * rank, 2 * rank)
        both = maps[pl.ds(at, rank)].astype(F32)
        put(at, both[:, :rank] + both[:, rank:] + coupling[classes[0, i]])

    levels = [[leaf[b] for b in range(boxes)]]
    while len(levels[-1]) > 2:
        levels.append(up(levels[-1], (t0, t1)))
    down = None
    paths = [None]
    for level in reversed(levels):
        across0 = dot3(jnp.concatenate(level[1::2], axis=0), s0)
        across1 = dot3(jnp.concatenate(level[0::2], axis=0), s1)
        if down is not None:
            parents = jnp.concatenate(down, axis=0)
            across0 = across0 + dot3(parents, t0, NT)
            across1 = across1 + dot3(parents, t1, NT)
        down = []
        for i in range(len(level) // 2):
            down.append(across0[i * columns : (i + 1) * columns])
            down.append(across1[i * columns : (i + 1) * columns])
        if paths[0] is None:
            paths = [t0.T, t1.T]
        else:
            tall = jnp.concatenate(paths, axis=0)
            left, right = dot3(tall, t0, NT), dot3(tall, t1, NT)
            paths = []
            for i in range(len(level) // 2):
                paths.append(left[i * rank : (i + 1) * rank])
                paths.append(right[i * rank : (i + 1) * rank])
    for b in range(boxes):
        local[:, b * rank : (b + 1) * rank] = down[b]
        high, low = split(paths[b])
        for half in range(2):
            rows = slice(half * rank, (half + 1) * rank)
            spread[rows, b * rank : (b + 1) * rank] = high
            spread[rows, (boxes + b) * rank : (boxes + b + 1) * rank] = low


def near_kernel(live, targets, sources, before, own, after, tiles, near, window):
    slots, points, _ = tiles.shape
    boxes = near.shape[0]
    for i, part in enumerate((before, own, after)):
        for b in range(boxes):
            window[i * boxes + b] = part[:, b * points : (b + 1) * points]
    near[...] = jnp.zeros_like(near)
    for slot in range(slots):
        source = window[sources[slot]]
        source = jnp.where(slot < live[0], source, jnp.zeros_like(source))
        target = targets[slot]
        near[target] = near[target] + dot(source, tiles[slot])


def field_kernel(gathered, maps, spread, local, basis, near, field):
    count = gathered.shape[0]
    boxes, rank, points = basis.shape
    pairs = count // 2
    wide = 4 * rank

    def step(k):
        coeffs = jnp.concatenate([gathered[2 * k], gathered[2 * k + 1]], axis=1)
        return dot(coeffs, maps[pl.ds(k * wide, wide)])

    if pairs <= 32:
        both = step(0)
        for k in range(1, pairs):
            both = both + step(k)
    else:
        both = lax.fori_loop(1, pairs, lambda k, sums: sums + step(k), step(0))
    summit = both[:, :rank] + both[:, rank:]
    doubled = dot(jnp.concatenate(split(summit), axis=1), spread[...])
    half = boxes * rank
    rounded = (doubled[:, :half] + doubled[:, half:] + local[...]).astype(BF16)
    for b in range(boxes):
        far = dot(rounded[:, b * rank : (b + 1) * rank], basis[b])
        field[:, b * points : (b + 1) * points] = near[b] + far


def call(kernel, name, outs, kinds, args, scratch=(), flops=0):
    spaces = {"v": pltpu.VMEM, "s": pltpu.SMEM}
    moved = sum(x.size * x.dtype.itemsize for x in args)
    return pl.pallas_call(
        kernel,
        name=name,
        out_shape=outs,
        in_specs=[pl.BlockSpec(memory_space=spaces[kind]) for kind in kinds],
        out_specs=jax.tree.map(lambda _: pl.BlockSpec(memory_space=pltpu.VMEM), outs),
        scratch_shapes=list(scratch),
        compiler_params=pltpu.CompilerParams(vmem_limit_bytes=VMEM_LIMIT),
        cost_estimate=pl.CostEstimate(flops=flops, bytes_accessed=moved, transcendentals=0),
    )(*args)


def body(
    vectors,
    leaf_basis,
    transfer,
    sibling_coupling,
    list_coupling,
    near_tiles,
    tile_target,
    tile_source,
    tile_count,
    couple_offset,
    couple_class,
):
    columns, width = vectors.shape
    boxes, rank, points = leaf_basis.shape
    count = lax.axis_size(AXES)
    bits = count.bit_length() - 1
    shape = jax.ShapeDtypeStruct

    def send(x, target):
        return lax.ppermute(x, AXES, [(i, target(i)) for i in range(count)])

    coeffs, leaf = call(
        leaf_kernel,
        "leaf",
        (shape((1, columns, 2 * rank), BF16), shape((boxes, columns, rank), F32)),
        "vvv",
        (vectors, leaf_basis, transfer),
    )
    before = send(vectors, lambda i: (i + 1) % count)
    after = send(vectors, lambda i: (i - 1) % count)
    device = lax.axis_index(AXES).astype(jnp.int32).reshape(1)
    maps, spread, local = call(
        functools.partial(map_kernel, bits),
        "maps",
        (
            shape((count * 2 * rank, 2 * rank), BF16),
            shape((2 * rank, 2 * boxes * rank), BF16),
            shape((columns, boxes * rank), F32),
        ),
        "sssvvvv",
        (device, couple_offset, couple_class, leaf, transfer, sibling_coupling, list_coupling),
        scratch=(pltpu.VMEM((count // 2 * rank, rank), F32),),
    )
    near = call(
        near_kernel,
        "near",
        shape((boxes, columns, points), F32),
        "sssvvvv",
        (tile_count, tile_target, tile_source, before, vectors, after, near_tiles),
        scratch=(pltpu.VMEM((3 * boxes, columns, points), BF16),),
    )
    gathered = coeffs
    for low, wide in rounds_of(bits):
        parts = [gathered]
        for step in range(1, 2**wide):
            parts.append(send(gathered, lambda i, mask=step << low: i ^ mask))
        gathered = jnp.concatenate(parts, axis=0)
    return call(
        field_kernel,
        "field",
        shape((columns, width), F32),
        "vvvvvv",
        (gathered, maps, spread, local, leaf_basis, near),
    )


def solution(mesh):
    in_specs = (
        P(None, AXES),
        P(AXES, None, None),
        P(),
        P(),
        P(),
        P(AXES, None, None),
        P(AXES),
        P(AXES),
        P(AXES),
        P(AXES, None),
        P(AXES, None),
    )
    return jax.shard_map(body, mesh=mesh, in_specs=in_specs, out_specs=P(None, AXES), check_vma=False)
```

```python
import functools

import jax
import jax.numpy as jnp
from jax import lax
from jax.experimental import pallas as pl
from jax.experimental.pallas import tpu as pltpu
from jax.sharding import PartitionSpec as P

AXES = ("leaf", "grp")
F32 = jnp.float32
BF16 = jnp.bfloat16
NN = (((1,), (0,)), ((), ()))
NT = (((1,), (1,)), ((), ()))
CHUNK = 512
VMEM_LIMIT = 48 * 2**20


def split(x):
    high = x.astype(BF16)
    return high, (x - high.astype(F32)).astype(BF16)


def dot(a, b, dims=NN):
    return lax.dot_general(a, b, dims, preferred_element_type=F32)


def dot3(a, b, dims=NN):
    a_high, a_low = split(a)
    b_high, b_low = split(b)
    return dot(a_high, b_high, dims) + (dot(a_low, b_high, dims) + dot(a_high, b_low, dims))


def rounds_of(bits):
    rounds = []
    top = bits
    while top > 0:
        wide = 2 if top > 1 else 1
        rounds.append((top - wide, wide))
        top -= wide
    return rounds


def masks_of(bits):
    masks = [0]
    for low, wide in rounds_of(bits):
        masks = [mask ^ (step << low) for step in range(2**wide) for mask in masks]
    return masks


def place_of(mask, bits):
    place, shift = 0, 0
    for low, wide in rounds_of(bits):
        place = place | (((mask >> low) & (2**wide - 1)) << shift)
        shift += wide
    return place


def up(blocks, transfer):
    left = jnp.concatenate(blocks[0::2], axis=0)
    right = jnp.concatenate(blocks[1::2], axis=0)
    rows = blocks[0].shape[0]
    total = dot3(left, transfer[0]) + dot3(right, transfer[1])
    return [total[i * rows : (i + 1) * rows] for i in range(len(blocks) // 2)]


def high_low(double):
    high, low = split(double)
    lane = lax.broadcasted_iota(jnp.int32, double.shape, 1)
    return jnp.where(lane < double.shape[1] // 2, high, low)


def leaf_kernel(vectors_hbm, basis_hbm, transfer_hbm, send, leaf, basis, paths, vectors, transfer, sems):
    boxes, rank, points = basis.shape
    columns = vectors.shape[0]
    steps = boxes.bit_length() - 1
    copies = [
        pltpu.make_async_copy(transfer_hbm, transfer, sems.at[0]),
        pltpu.make_async_copy(vectors_hbm, vectors, sems.at[1]),
        pltpu.make_async_copy(basis_hbm, basis, sems.at[2]),
    ]
    for copy in copies:
        copy.start()
    copies[0].wait()
    t0, t1 = transfer[0], transfer[1]
    stack = jnp.concatenate([t0, t1], axis=0)
    for height in range(1, steps):
        paths[height - 1, : 2**height * rank, :rank] = stack
        stack = jnp.concatenate([dot3(stack, t0), dot3(stack, t1)], axis=0)
    double = jnp.concatenate([stack, stack], axis=1)
    paths[steps - 1] = double
    weights, rest = split(double)
    copies[1].wait()
    copies[2].wait()
    high, low = [], []
    for b in range(boxes):
        coeffs = dot(vectors[:, b * points : (b + 1) * points], basis[b], NT)
        leaf[b] = coeffs
        one, other = split(coeffs)
        high.append(one)
        low.append(other)
    high = jnp.concatenate(high, axis=1)
    low = jnp.concatenate(low, axis=1)
    send[0] = high_low(dot(high, weights) + (dot(low, weights) + dot(high, rest)))


def map_kernel(
    bits,
    device,
    offsets_hbm,
    classes_hbm,
    targets_hbm,
    sources_hbm,
    live_hbm,
    transfer_hbm,
    sibling_hbm,
    coupling_hbm,
    tiles_hbm,
    coeffs,
    leaf,
    paths,
    maps,
    spread,
    local,
    tiles,
    passed,
    targets,
    sources,
    live,
    offsets,
    classes,
    transfer,
    sibling,
    coupling,
    sems,
):
    boxes, columns, rank = leaf.shape
    pairs = (
        (transfer_hbm, transfer),
        (sibling_hbm, sibling),
        (offsets_hbm, offsets),
        (classes_hbm, classes),
        (coupling_hbm, coupling),
        (targets_hbm, targets),
        (sources_hbm, sources),
        (live_hbm, live),
        (tiles_hbm, tiles),
    )
    copies = [pltpu.make_async_copy(a, b, sems.at[i]) for i, (a, b) in enumerate(pairs)]
    for copy in copies:
        copy.start()
    passed[...] = coeffs[...]
    me = device[0]
    count = 2**bits
    steps = boxes.bit_length() - 1
    copies[0].wait()
    copies[1].wait()
    t0, t1 = transfer[0], transfer[1]
    s0, s1 = sibling[0], sibling[1]

    def put(at, double):
        both = high_low(double)
        at = pl.multiple_of(at * 2 * rank, 2 * rank)
        maps[pl.ds(at, rank)] = both
        maps[pl.ds(at + rank, rank)] = both

    def twice(x):
        return jnp.concatenate([x, x], axis=1)

    def place(height, low):
        return place_of((1 << height) | (low ^ (me & ((1 << height) - 1))), bits)

    def path(height):
        if height <= steps:
            at = pl.multiple_of((me & ((1 << height) - 1)) * rank, rank)
            return paths[height - 1, pl.ds(at, rank), :rank]
        return dot3(path(height - 1), transfer[(me >> (height - 1)) & 1])

    put(0, jnp.zeros((rank, 2 * rank), F32))
    for height in range(bits):
        mine = sibling[(me >> height) & 1]
        if height == 0:
            put(place(0, 0), twice(mine))
            continue
        bridge = twice(dot3(mine, path(height), NT))
        base = min(height, steps)
        fans = [bridge]
        for step in range(height - 1, base - 1, -1):
            fans = [dot3(t, fan) for fan in fans for t in (t0, t1)]
        rows = 2**base * rank
        for j, fan in enumerate(fans):
            block = dot3(paths[base - 1, :rows, :rank], fan)
            for i in range(2**base):
                put(place(height, (j << base) + i), block[i * rank : (i + 1) * rank])
    copies[2].wait()
    copies[3].wait()
    copies[4].wait()
    for i in range(offsets.shape[1]):
        mask = ((me + offsets[0, i] + count) & (count - 1)) ^ me
        at = place_of(mask, bits)
        both = maps[pl.ds(pl.multiple_of(at * 2 * rank, 2 * rank), rank)].astype(F32)
        put(at, twice(both[:, :rank] + both[:, rank:] + coupling[classes[0, i]]))

    half = boxes * rank
    high, low = split(paths[steps - 1])
    spread[:half] = high
    spread[half:] = low
    levels = [[leaf[b] for b in range(boxes)]]
    while len(levels[-1]) > 2:
        levels.append(up(levels[-1], (t0, t1)))
    down = None
    for level in reversed(levels):
        across0 = dot3(jnp.concatenate(level[1::2], axis=0), s0)
        across1 = dot3(jnp.concatenate(level[0::2], axis=0), s1)
        if down is not None:
            parents = jnp.concatenate(down, axis=0)
            across0 = across0 + dot3(parents, t0, NT)
            across1 = across1 + dot3(parents, t1, NT)
        down = []
        for i in range(len(level) // 2):
            down.append(across0[i * columns : (i + 1) * columns])
            down.append(across1[i * columns : (i + 1) * columns])
    for b in range(boxes):
        local[:, b * rank : (b + 1) * rank] = down[b]
    for copy in copies[5:]:
        copy.wait()


def near_kernel(live, targets, sources, before, own, after, tiles, near, window):
    slots, points, _ = tiles.shape
    boxes = near.shape[0]
    for i, part in enumerate((before, own, after)):
        for b in range(boxes):
            window[i * boxes + b] = part[:, b * points : (b + 1) * points]
    near[...] = jnp.zeros_like(near)
    for slot in range(slots):
        source = window[sources[slot]]
        source = jnp.where(slot < live[0], source, jnp.zeros_like(source))
        target = targets[slot]
        near[target] = near[target] + dot(source, tiles[slot])


def field_kernel(gathered, maps, spread, local, basis, near, field):
    count = gathered.shape[0]
    boxes, rank, points = basis.shape
    pairs = count // 2
    wide = 4 * rank

    def step(k):
        coeffs = jnp.concatenate([gathered[2 * k], gathered[2 * k + 1]], axis=1)
        return dot(coeffs, maps[pl.ds(k * wide, wide)])

    if pairs <= 32:
        both = step(0)
        for k in range(1, pairs):
            both = both + step(k)
    else:
        both = lax.fori_loop(1, pairs, lambda k, sums: sums + step(k), step(0))
    summit = both[:, :rank] + both[:, rank:]
    doubled = dot(jnp.concatenate(split(summit), axis=1), spread[...], NT)
    half = boxes * rank
    rounded = (doubled[:, :half] + doubled[:, half:] + local[...]).astype(BF16)
    for b in range(boxes):
        far = dot(rounded[:, b * rank : (b + 1) * rank], basis[b])
        field[:, b * points : (b + 1) * points] = near[b] + far


SPACES = {"v": pltpu.VMEM, "s": pltpu.SMEM, "h": pltpu.HBM}


def call(kernel, name, kinds, args, outs, scratch=(), flops=0):
    moved = sum(x.size * x.dtype.itemsize for x in args)
    return pl.pallas_call(
        kernel,
        name=name,
        out_shape=[jax.ShapeDtypeStruct(shape, kind) for _, shape, kind in outs],
        in_specs=[pl.BlockSpec(memory_space=SPACES[kind]) for kind in kinds],
        out_specs=[pl.BlockSpec(memory_space=SPACES[space]) for space, _, _ in outs],
        scratch_shapes=list(scratch),
        compiler_params=pltpu.CompilerParams(vmem_limit_bytes=VMEM_LIMIT),
        cost_estimate=pl.CostEstimate(flops=flops, bytes_accessed=moved, transcendentals=0),
    )(*args)


def body(
    vectors,
    leaf_basis,
    transfer,
    sibling_coupling,
    list_coupling,
    near_tiles,
    tile_target,
    tile_source,
    tile_count,
    couple_offset,
    couple_class,
):
    columns, width = vectors.shape
    boxes, rank, points = leaf_basis.shape
    count = lax.axis_size(AXES)
    bits = count.bit_length() - 1
    steps = boxes.bit_length() - 1
    double = 2 * rank
    dma = pltpu.SemaphoreType.DMA

    def send(x, target):
        return lax.ppermute(x, AXES, [(i, target(i)) for i in range(count)])

    def swap(x, mask):
        return send(x, lambda i: i ^ mask)

    before = send(vectors, lambda i: (i + 1) % count)
    coeffs, leaf, basis, paths = call(
        leaf_kernel,
        "leaf",
        "hhh",
        (vectors, leaf_basis, transfer),
        (
            ("v", (1, columns, double), BF16),
            ("v", (boxes, columns, rank), F32),
            ("v", leaf_basis.shape, BF16),
            ("v", (steps, boxes * rank, double), F32),
        ),
        scratch=(pltpu.VMEM(vectors.shape, BF16), pltpu.VMEM(transfer.shape, F32), dma((3,))),
    )
    device = lax.axis_index(AXES).astype(jnp.int32).reshape(1)
    ints = jnp.int32
    maps, spread, local, tiles, passed, targets, sources, live = call(
        functools.partial(map_kernel, bits),
        "maps",
        "shhhhhhhhhvvv",
        (
            device,
            couple_offset,
            couple_class,
            tile_target,
            tile_source,
            tile_count,
            transfer,
            sibling_coupling,
            list_coupling,
            near_tiles,
            coeffs,
            leaf,
            paths,
        ),
        (
            ("v", (count * double, double), BF16),
            ("v", (2 * boxes * rank, double), BF16),
            ("v", (columns, boxes * rank), F32),
            ("v", near_tiles.shape, BF16),
            ("v", coeffs.shape, BF16),
            ("s", tile_target.shape, ints),
            ("s", tile_source.shape, ints),
            ("s", tile_count.shape, ints),
        ),
        scratch=(
            pltpu.SMEM(couple_offset.shape, ints),
            pltpu.SMEM(couple_class.shape, ints),
            pltpu.VMEM(transfer.shape, F32),
            pltpu.VMEM(sibling_coupling.shape, F32),
            pltpu.VMEM(list_coupling.shape, F32),
            dma((9,)),
        ),
    )
    gathered = coeffs
    after = None
    for index, (low, wide) in enumerate(rounds_of(bits)):
        parts = [passed if index == 0 else gathered]
        for step in range(1, 2**wide):
            parts.append(swap(gathered, step << low))
        gathered = jnp.concatenate(parts, axis=0)
        if index == 0:
            gathered, late = lax.optimization_barrier((gathered, vectors))
            after = send(late, lambda i: (i - 1) % count)
    (near,) = call(
        near_kernel,
        "near",
        "sssvvvv",
        (live, targets, sources, before, vectors, after, tiles),
        (("v", (boxes, columns, points), F32),),
        scratch=(pltpu.VMEM((3 * boxes, columns, points), BF16),),
    )
    (field,) = call(
        field_kernel,
        "field",
        "vvvvvv",
        (gathered, maps, spread, local, basis, near),
        (("v", (columns, width), F32),),
    )
    return field


def solution(mesh):
    in_specs = (
        P(None, AXES),
        P(AXES, None, None),
        P(),
        P(),
        P(),
        P(AXES, None, None),
        P(AXES),
        P(AXES),
        P(AXES),
        P(AXES, None),
        P(AXES, None),
    )
    return jax.shard_map(body, mesh=mesh, in_specs=in_specs, out_specs=P(None, AXES), check_vma=False)
```

```python
import functools

import jax
import jax.numpy as jnp
from jax import lax
from jax.experimental import pallas as pl
from jax.experimental.pallas import tpu as pltpu
from jax.sharding import PartitionSpec as P

AXES = ("leaf", "grp")
F32 = jnp.float32
BF16 = jnp.bfloat16
NN = (((1,), (0,)), ((), ()))
NT = (((1,), (1,)), ((), ()))
CHUNK = 512
VMEM_LIMIT = 48 * 2**20


def split(x):
    high = x.astype(BF16)
    return high, (x - high.astype(F32)).astype(BF16)


def dot(a, b, dims=NN):
    return lax.dot_general(a, b, dims, preferred_element_type=F32)


def dot3(a, b, dims=NN):
    a_high, a_low = split(a)
    b_high, b_low = split(b)
    return dot(a_high, b_high, dims) + (dot(a_low, b_high, dims) + dot(a_high, b_low, dims))


def rounds_of(bits):
    rounds = []
    top = bits
    while top > 0:
        wide = 2 if top > 1 else 1
        rounds.append((top - wide, wide))
        top -= wide
    return rounds


def masks_of(bits):
    masks = [0]
    for low, wide in rounds_of(bits):
        masks = [mask ^ (step << low) for step in range(2**wide) for mask in masks]
    return masks


def place_of(mask, bits):
    place, shift = 0, 0
    for low, wide in rounds_of(bits):
        place = place | (((mask >> low) & (2**wide - 1)) << shift)
        shift += wide
    return place


def up(blocks, transfer):
    left = jnp.concatenate(blocks[0::2], axis=0)
    right = jnp.concatenate(blocks[1::2], axis=0)
    rows = blocks[0].shape[0]
    total = dot3(left, transfer[0]) + dot3(right, transfer[1])
    return [total[i * rows : (i + 1) * rows] for i in range(len(blocks) // 2)]


def high_low(double):
    high, low = split(double)
    lane = lax.broadcasted_iota(jnp.int32, double.shape, 1)
    return jnp.where(lane < double.shape[1] // 2, high, low)


def leaf_kernel(vectors_hbm, basis_hbm, transfer_hbm, send, leaf, basis, paths, vectors, transfer, sems):
    boxes, rank, points = basis.shape
    columns = vectors.shape[0]
    steps = boxes.bit_length() - 1
    copies = [
        pltpu.make_async_copy(transfer_hbm, transfer, sems.at[0]),
        pltpu.make_async_copy(vectors_hbm, vectors, sems.at[1]),
        pltpu.make_async_copy(basis_hbm, basis, sems.at[2]),
    ]
    for copy in copies:
        copy.start()
    copies[0].wait()
    t0, t1 = transfer[0], transfer[1]
    stack = jnp.concatenate([t0, t1], axis=0)
    for height in range(1, steps):
        paths[height - 1, : 2**height * rank, :rank] = stack
        stack = jnp.concatenate([dot3(stack, t0), dot3(stack, t1)], axis=0)
    double = jnp.concatenate([stack, stack], axis=1)
    paths[steps - 1] = double
    weights, rest = split(double)
    copies[1].wait()
    copies[2].wait()
    high, low = [], []
    for b in range(boxes):
        coeffs = dot(vectors[:, b * points : (b + 1) * points], basis[b], NT)
        leaf[b] = coeffs
        one, other = split(coeffs)
        high.append(one)
        low.append(other)
    high = jnp.concatenate(high, axis=1)
    low = jnp.concatenate(low, axis=1)
    send[0] = high_low(dot(high, weights) + (dot(low, weights) + dot(high, rest)))


def map_kernel(
    bits,
    device,
    offsets_hbm,
    classes_hbm,
    targets_hbm,
    sources_hbm,
    transfer_hbm,
    sibling_hbm,
    coupling_hbm,
    tiles_hbm,
    coeffs,
    leaf,
    paths,
    maps,
    spread,
    local,
    tiles,
    passed,
    targets,
    sources,
    offsets,
    classes,
    transfer,
    sibling,
    coupling,
    sems,
):
    boxes, columns, rank = leaf.shape
    pairs = (
        (transfer_hbm, transfer),
        (sibling_hbm, sibling),
        (offsets_hbm, offsets),
        (classes_hbm, classes),
        (coupling_hbm, coupling),
        (targets_hbm, targets),
        (sources_hbm, sources),
        (tiles_hbm, tiles),
    )
    copies = [pltpu.make_async_copy(a, b, sems.at[i]) for i, (a, b) in enumerate(pairs)]
    for copy in copies:
        copy.start()
    passed[...] = coeffs[...]
    me = device[0]
    count = 2**bits
    steps = boxes.bit_length() - 1
    copies[0].wait()
    copies[1].wait()
    t0, t1 = transfer[0], transfer[1]
    s0, s1 = sibling[0], sibling[1]

    def put(at, double):
        both = high_low(double)
        at = pl.multiple_of(at * 2 * rank, 2 * rank)
        maps[pl.ds(at, rank)] = both
        maps[pl.ds(at + rank, rank)] = both

    def twice(x):
        return jnp.concatenate([x, x], axis=1)

    def place(height, low):
        return place_of((1 << height) | (low ^ (me & ((1 << height) - 1))), bits)

    def path(height):
        if height <= steps:
            at = pl.multiple_of((me & ((1 << height) - 1)) * rank, rank)
            return paths[height - 1, pl.ds(at, rank), :rank]
        return dot3(path(height - 1), transfer[(me >> (height - 1)) & 1])

    put(0, jnp.zeros((rank, 2 * rank), F32))
    for height in range(bits):
        mine = sibling[(me >> height) & 1]
        if height == 0:
            put(place(0, 0), twice(mine))
            continue
        bridge = twice(dot3(mine, path(height), NT))
        base = min(height, steps)
        fans = [bridge]
        for step in range(height - 1, base - 1, -1):
            fans = [dot3(t, fan) for fan in fans for t in (t0, t1)]
        rows = 2**base * rank
        for j, fan in enumerate(fans):
            block = dot3(paths[base - 1, :rows, :rank], fan)
            for i in range(2**base):
                put(place(height, (j << base) + i), block[i * rank : (i + 1) * rank])
    copies[2].wait()
    copies[3].wait()
    copies[4].wait()
    for i in range(offsets.shape[1]):
        mask = ((me + offsets[0, i] + count) & (count - 1)) ^ me
        at = place_of(mask, bits)
        both = maps[pl.ds(pl.multiple_of(at * 2 * rank, 2 * rank), rank)].astype(F32)
        put(at, twice(both[:, :rank] + both[:, rank:] + coupling[classes[0, i]]))

    half = boxes * rank
    high, low = split(paths[steps - 1])
    spread[:half] = high
    spread[half:] = low
    levels = [[leaf[b] for b in range(boxes)]]
    while len(levels[-1]) > 2:
        levels.append(up(levels[-1], (t0, t1)))
    down = None
    for level in reversed(levels):
        across0 = dot3(jnp.concatenate(level[1::2], axis=0), s0)
        across1 = dot3(jnp.concatenate(level[0::2], axis=0), s1)
        if down is not None:
            parents = jnp.concatenate(down, axis=0)
            across0 = across0 + dot3(parents, t0, NT)
            across1 = across1 + dot3(parents, t1, NT)
        down = []
        for i in range(len(level) // 2):
            down.append(across0[i * columns : (i + 1) * columns])
            down.append(across1[i * columns : (i + 1) * columns])
    for b in range(boxes):
        local[:, b * rank : (b + 1) * rank] = down[b]
    for copy in copies[5:]:
        copy.wait()


def near_kernel(live, targets, sources, before, own, after, tiles, near, window):
    slots, points, _ = tiles.shape
    boxes = near.shape[0]
    for i, part in enumerate((before, own, after)):
        for b in range(boxes):
            window[i * boxes + b] = part[:, b * points : (b + 1) * points]
    near[...] = jnp.zeros_like(near)
    for slot in range(slots):
        source = window[sources[slot]]
        source = jnp.where(slot < live[0], source, jnp.zeros_like(source))
        target = targets[slot]
        near[target] = near[target] + dot(source, tiles[slot])


def field_kernel(gathered, maps, spread, local, basis, near, field):
    count = gathered.shape[0]
    boxes, rank, points = basis.shape
    pairs = count // 2
    wide = 4 * rank

    def step(k):
        coeffs = jnp.concatenate([gathered[2 * k], gathered[2 * k + 1]], axis=1)
        return dot(coeffs, maps[pl.ds(k * wide, wide)])

    if pairs <= 32:
        both = step(0)
        for k in range(1, pairs):
            both = both + step(k)
    else:
        both = lax.fori_loop(1, pairs, lambda k, sums: sums + step(k), step(0))
    summit = both[:, :rank] + both[:, rank:]
    doubled = dot(jnp.concatenate(split(summit), axis=1), spread[...], NT)
    half = boxes * rank
    rounded = (doubled[:, :half] + doubled[:, half:] + local[...]).astype(BF16)
    for b in range(boxes):
        far = dot(rounded[:, b * rank : (b + 1) * rank], basis[b])
        field[:, b * points : (b + 1) * points] = near[b] + far


SPACES = {"v": pltpu.VMEM, "s": pltpu.SMEM, "h": pl.ANY}


def call(kernel, name, kinds, args, outs, scratch=(), flops=0):
    moved = sum(x.size * x.dtype.itemsize for x in args)
    args = [
        pltpu.with_memory_space_constraint(x, pltpu.HBM) if kind == "h" else x
        for kind, x in zip(kinds, args)
    ]
    return pl.pallas_call(
        kernel,
        name=name,
        out_shape=[jax.ShapeDtypeStruct(shape, kind) for _, shape, kind in outs],
        in_specs=[pl.BlockSpec(memory_space=SPACES[kind]) for kind in kinds],
        out_specs=[pl.BlockSpec(memory_space=SPACES[space]) for space, _, _ in outs],
        scratch_shapes=list(scratch),
        compiler_params=pltpu.CompilerParams(vmem_limit_bytes=VMEM_LIMIT),
        cost_estimate=pl.CostEstimate(flops=flops, bytes_accessed=moved, transcendentals=0),
    )(*args)


def body(
    vectors,
    leaf_basis,
    transfer,
    sibling_coupling,
    list_coupling,
    near_tiles,
    tile_target,
    tile_source,
    tile_count,
    couple_offset,
    couple_class,
):
    columns, width = vectors.shape
    boxes, rank, points = leaf_basis.shape
    count = lax.axis_size(AXES)
    bits = count.bit_length() - 1
    steps = boxes.bit_length() - 1
    double = 2 * rank
    dma = pltpu.SemaphoreType.DMA

    def send(x, target):
        return lax.ppermute(x, AXES, [(i, target(i)) for i in range(count)])

    def swap(x, mask):
        return send(x, lambda i: i ^ mask)

    before = send(vectors, lambda i: (i + 1) % count)
    coeffs, leaf, basis, paths, own = call(
        leaf_kernel,
        "leaf",
        "hhh",
        (vectors, leaf_basis, transfer),
        (
            ("v", (1, columns, double), BF16),
            ("v", (boxes, columns, rank), F32),
            ("v", leaf_basis.shape, BF16),
            ("v", (steps, boxes * rank, double), F32),
            ("v", vectors.shape, BF16),
        ),
        scratch=(pltpu.VMEM(transfer.shape, F32), dma((3,))),
    )
    device = lax.axis_index(AXES).astype(jnp.int32).reshape(1)
    ints = jnp.int32
    maps, spread, local, tiles, passed, targets, sources = call(
        functools.partial(map_kernel, bits),
        "maps",
        "shhhhhhhhvvv",
        (
            device,
            couple_offset,
            couple_class,
            tile_target,
            tile_source,
            transfer,
            sibling_coupling,
            list_coupling,
            near_tiles,
            coeffs,
            leaf,
            paths,
        ),
        (
            ("v", (count * double, double), BF16),
            ("v", (2 * boxes * rank, double), BF16),
            ("v", (columns, boxes * rank), F32),
            ("v", near_tiles.shape, BF16),
            ("v", coeffs.shape, BF16),
            ("s", tile_target.shape, ints),
            ("s", tile_source.shape, ints),
        ),
        scratch=(
            pltpu.SMEM(couple_offset.shape, ints),
            pltpu.SMEM(couple_class.shape, ints),
            pltpu.VMEM(transfer.shape, F32),
            pltpu.VMEM(sibling_coupling.shape, F32),
            pltpu.VMEM(list_coupling.shape, F32),
            dma((8,)),
        ),
    )
    gathered = coeffs
    after = None
    for index, (low, wide) in enumerate(rounds_of(bits)):
        parts = [passed if index == 0 else gathered]
        for step in range(1, 2**wide):
            parts.append(swap(gathered, step << low))
        gathered = jnp.concatenate(parts, axis=0)
        if index == 0:
            gathered, late = lax.optimization_barrier((gathered, vectors))
            after = send(late, lambda i: (i - 1) % count)
    (near,) = call(
        near_kernel,
        "near",
        "sssvvvv",
        (tile_count, targets, sources, before, own, after, tiles),
        (("v", (boxes, columns, points), F32),),
        scratch=(pltpu.VMEM((3 * boxes, columns, points), BF16),),
    )
    (field,) = call(
        field_kernel,
        "field",
        "vvvvvv",
        (gathered, maps, spread, local, basis, near),
        (("v", (columns, width), F32),),
    )
    return field


def solution(mesh):
    in_specs = (
        P(None, AXES),
        P(AXES, None, None),
        P(),
        P(),
        P(),
        P(AXES, None, None),
        P(AXES),
        P(AXES),
        P(AXES),
        P(AXES, None),
        P(AXES, None),
    )
    return jax.shard_map(body, mesh=mesh, in_specs=in_specs, out_specs=P(None, AXES), check_vma=False)
```

```python
import functools

import jax
import jax.numpy as jnp
from jax import lax
from jax.experimental import pallas as pl
from jax.experimental.pallas import tpu as pltpu
from jax.sharding import PartitionSpec as P

AXES = ("leaf", "grp")
F32 = jnp.float32
BF16 = jnp.bfloat16
NN = (((1,), (0,)), ((), ()))
NT = (((1,), (1,)), ((), ()))
CHUNK = 512
STACK = 6 * 2**20


def split(x):
    high = x.astype(BF16)
    return high, (x - high.astype(F32)).astype(BF16)


def dot(a, b, dims=NN):
    return lax.dot_general(a, b, dims, preferred_element_type=F32)


def dot3(a, b, dims=NN):
    a_high, a_low = split(a)
    b_high, b_low = split(b)
    return dot(a_high, b_high, dims) + (dot(a_low, b_high, dims) + dot(a_high, b_low, dims))


def rounds_of(bits):
    rounds = []
    top = bits
    while top > 0:
        wide = 2 if top > 1 else 1
        rounds.append((top - wide, wide))
        top -= wide
    return rounds


def masks_of(bits):
    masks = [0]
    for low, wide in rounds_of(bits):
        masks = [mask ^ (step << low) for step in range(2**wide) for mask in masks]
    return masks


def place_of(mask, bits):
    place, shift = 0, 0
    for low, wide in rounds_of(bits):
        place = place | (((mask >> low) & (2**wide - 1)) << shift)
        shift += wide
    return place


def up(blocks, transfer):
    left = jnp.concatenate(blocks[0::2], axis=0)
    right = jnp.concatenate(blocks[1::2], axis=0)
    rows = blocks[0].shape[0]
    total = dot3(left, transfer[0]) + dot3(right, transfer[1])
    return [total[i * rows : (i + 1) * rows] for i in range(len(blocks) // 2)]


def high_low(double):
    high, low = split(double)
    lane = lax.broadcasted_iota(jnp.int32, double.shape, 1)
    return jnp.where(lane < double.shape[1] // 2, high, low)


def start_copies(pairs, sems):
    copies = [pltpu.make_async_copy(a, b, sems.at[i]) for i, (a, b) in enumerate(pairs)]
    for copy in copies:
        copy.start()
    return copies


def leaf_kernel(transfer_hbm, vectors_hbm, sibling_hbm, basis_hbm, transfer, vectors, sibling, send, leaf, *refs):
    *paths, basis, sems = refs
    boxes, rank, points = basis.shape
    steps = boxes.bit_length() - 1
    pairs = ((transfer_hbm, transfer), (vectors_hbm, vectors), (basis_hbm, basis), (sibling_hbm, sibling))
    copies = start_copies(pairs, sems)
    copies[0].wait()
    t0, t1 = transfer[0], transfer[1]
    stack = jnp.concatenate([t0, t1], axis=0)
    for height in range(1, steps):
        paths[height - 1][...] = jnp.concatenate([stack, stack], axis=1)
        stack = jnp.concatenate([dot3(stack, t0), dot3(stack, t1)], axis=0)
    double = jnp.concatenate([stack, stack], axis=1)
    paths[steps - 1][...] = double
    weights, rest = split(double)
    copies[1].wait()
    copies[2].wait()
    high, low = [], []
    for b in range(boxes):
        coeffs = dot(vectors[:, b * points : (b + 1) * points], basis[b], NT)
        leaf[b] = coeffs
        one, other = split(coeffs)
        high.append(one)
        low.append(other)
    high = jnp.concatenate(high, axis=1)
    low = jnp.concatenate(low, axis=1)
    send[0] = high_low(dot(high, weights) + (dot(low, weights) + dot(high, rest)))
    copies[3].wait()


def down_kernel(coeffs, leaf, paths, transfer, sibling, before, spread, local, passed):
    boxes, columns, rank = leaf.shape
    half = boxes * rank
    passed[...] = coeffs[...]
    high, low = split(paths[...])
    spread[:half] = high
    spread[half:] = low
    t0, t1 = transfer[0], transfer[1]
    levels = [[leaf[b] for b in range(boxes)]]
    while len(levels[-1]) > 2:
        levels.append(up(levels[-1], (t0, t1)))
    s0, s1 = sibling[0], sibling[1]
    down = None
    for level in reversed(levels):
        across0 = dot3(jnp.concatenate(level[1::2], axis=0), s0)
        across1 = dot3(jnp.concatenate(level[0::2], axis=0), s1)
        if down is not None:
            parents = jnp.concatenate(down, axis=0)
            across0 = across0 + dot3(parents, t0, NT)
            across1 = across1 + dot3(parents, t1, NT)
        down = []
        for i in range(len(level) // 2):
            down.append(across0[i * columns : (i + 1) * columns])
            down.append(across1[i * columns : (i + 1) * columns])
    for b in range(boxes):
        local[:, b * rank : (b + 1) * rank] = down[b]


def map_kernel(bits, device, *refs):
    hbm, (gathered, transfer, sibling), paths = refs[:5], refs[5:8], refs[8:-9]
    maps, passed, places, *here, sems = refs[-9:]
    copies = start_copies(zip(hbm, here), sems)
    _, _, offsets, classes, coupling = here
    rank = transfer.shape[1]
    passed[...] = gathered[...]
    me = device[0]
    count = 2**bits
    steps = len(paths)
    boxes = 2**steps

    def put(at, double):
        both = high_low(double)
        if not isinstance(at, int):
            at = pl.multiple_of(at * 2 * rank, 2 * rank)
        else:
            at = at * 2 * rank
        maps[pl.ds(at, rank)] = both
        maps[pl.ds(at + rank, rank)] = both

    def twice(x):
        return jnp.concatenate([x, x], axis=1)

    def place(height, low):
        return place_of((1 << height) | (low ^ (me & ((1 << height) - 1))), bits)

    sides = []
    for height in range(1, steps + 1):
        tall = paths[height - 1][...]
        sides.append(jnp.concatenate([high_low(tall), tall.astype(BF16)], axis=1))

    def climb(height, fan):
        fan_high, fan_low = split(fan)
        weights = jnp.concatenate([fan_high, fan_high, fan_low, jnp.zeros_like(fan_low)], axis=0)
        return dot(sides[height - 1], weights)

    t0, t1 = transfer[0], transfer[1]

    def path(height):
        if height <= steps:
            at = pl.multiple_of((me & ((1 << height) - 1)) * rank, rank)
            return paths[height - 1][pl.ds(at, rank), :rank]
        return dot3(path(height - 1), transfer[(me >> (height - 1)) & 1])

    wide = []
    for height in range(1, bits):
        mine = sibling[(me >> height) & 1]
        bridge = twice(dot3(mine, path(height), NT))
        fans = [bridge]
        for step in range(height - 1, steps - 1, -1):
            fans = [dot3(t, fan) for fan in fans for t in (t0, t1)]
        if height < steps:
            block = climb(height, bridge)
            for i in range(2**height):
                put(place(height, i), block[i * rank : (i + 1) * rank])
        else:
            wide += [(height, j, fan) for j, fan in enumerate(fans)]
    for start in range(0, len(wide), 4):
        part = wide[start : start + 4]
        block = climb(steps, jnp.concatenate([fan for _, _, fan in part], axis=1))
        for k, (height, j, _) in enumerate(part):
            for i in range(boxes):
                one = block[i * rank : (i + 1) * rank, k * 2 * rank : (k + 1) * 2 * rank]
                put(place(height, (j << steps) + i), one)
    put(0, jnp.zeros((rank, 2 * rank), F32))
    put(place(0, 0), twice(sibling[me & 1]))
    for copy in copies:
        copy.wait()
    lane = lax.broadcasted_iota(jnp.int32, offsets.shape, 1)
    for i in range(offsets.shape[1]):
        offset = jnp.sum(jnp.where(lane == i, offsets[...], 0))
        kind = jnp.sum(jnp.where(lane == i, classes[...], 0))
        link = place_of(((me + offset + count) & (count - 1)) ^ me, bits)
        places[i] = jnp.full(places.shape[1:], link, jnp.int32)
        put(count + i, twice(coupling[kind]))


def near_kernel(live, targets, sources, before, own, after, tiles, gathered, near, window):
    slots, points, _ = tiles.shape
    boxes = near.shape[0]
    for i, part in enumerate((before, own, after)):
        for b in range(boxes):
            window[i * boxes + b] = part[:, b * points : (b + 1) * points]
    near[...] = jnp.zeros_like(near)
    for slot in range(slots):
        source = window[sources[slot]]
        source = jnp.where(slot < live[0], source, jnp.zeros_like(source))
        target = targets[slot]
        near[target] = near[target] + dot(source, tiles[slot])


def field_kernel(places, gathered, maps, spread, local, basis, near, field):
    count = gathered.shape[0]
    boxes, rank, points = basis.shape
    pairs = count // 2
    wide = 4 * rank

    def step(k):
        coeffs = jnp.concatenate([gathered[2 * k], gathered[2 * k + 1]], axis=1)
        return dot(coeffs, maps[pl.ds(k * wide, wide)])

    if pairs <= 32:
        both = step(0)
        for k in range(1, pairs):
            both = both + step(k)
    else:
        both = lax.fori_loop(1, pairs, lambda k, sums: sums + step(k), step(0))
    for i in range(places.shape[0]):
        rows = slice((count + i) * 2 * rank, (count + i + 1) * 2 * rank)
        both = both + dot(gathered[jnp.max(places[i])], maps[rows])
    summit = both[:, :rank] + both[:, rank:]
    doubled = dot(jnp.concatenate(split(summit), axis=1), spread[...], NT)
    half = boxes * rank
    rounded = (doubled[:, :half] + doubled[:, half:] + local[...]).astype(BF16)
    for b in range(boxes):
        far = dot(rounded[:, b * rank : (b + 1) * rank], basis[b])
        field[:, b * points : (b + 1) * points] = near[b] + far


SPACES = {"v": pltpu.VMEM, "s": pltpu.SMEM, "h": pl.ANY}


def call(kernel, name, kinds, args, outs, scratch=(), flops=0):
    moved = sum(x.size * x.dtype.itemsize for x in args)
    held = [x for x, kind in zip(args, kinds) if kind == "v"]
    held += [jax.ShapeDtypeStruct(shape, kind) for space, shape, kind in outs if space == "v"]
    limit = STACK + sum(x.size // x.shape[-1] * max(x.shape[-1], 128) * x.dtype.itemsize for x in held)
    args = [
        pltpu.with_memory_space_constraint(x, pltpu.HBM) if kind == "h" else x
        for kind, x in zip(kinds, args)
    ]
    return pl.pallas_call(
        kernel,
        name=name,
        out_shape=[jax.ShapeDtypeStruct(shape, kind) for _, shape, kind in outs],
        in_specs=[pl.BlockSpec(memory_space=SPACES[kind]) for kind in kinds],
        out_specs=[pl.BlockSpec(memory_space=SPACES[space]) for space, _, _ in outs],
        scratch_shapes=list(scratch),
        compiler_params=pltpu.CompilerParams(vmem_limit_bytes=limit),
        cost_estimate=pl.CostEstimate(flops=flops, bytes_accessed=moved, transcendentals=0),
    )(*args)


def body(
    vectors,
    leaf_basis,
    transfer,
    sibling_coupling,
    list_coupling,
    near_tiles,
    tile_target,
    tile_source,
    tile_count,
    couple_offset,
    couple_class,
):
    columns, width = vectors.shape
    boxes, rank, points = leaf_basis.shape
    count = lax.axis_size(AXES)
    bits = count.bit_length() - 1
    steps = boxes.bit_length() - 1
    double = 2 * rank
    dma = pltpu.SemaphoreType.DMA

    def send(x, target):
        return lax.ppermute(x, AXES, [(i, target(i)) for i in range(count)])

    def swap(x, mask):
        return send(x, lambda i: i ^ mask)

    before = send(vectors, lambda i: (i + 1) % count)
    ints = jnp.int32
    plain = (transfer, vectors, sibling_coupling)
    transfer, own, sibling, coeffs, leaf, *paths = call(
        leaf_kernel,
        "leaf",
        "hhhh",
        (*plain, leaf_basis),
        (
            *(("v", x.shape, x.dtype) for x in plain),
            ("v", (1, columns, double), BF16),
            ("v", (boxes, columns, rank), F32),
            *(("v", (2**height * rank, double), F32) for height in range(1, steps + 1)),
        ),
        scratch=(pltpu.VMEM(leaf_basis.shape, BF16), dma((4,))),
    )
    device = lax.axis_index(AXES).astype(ints).reshape(1)
    spread, local, passed = call(
        down_kernel,
        "down",
        "vvvvvv",
        (coeffs, leaf, paths[-1], transfer, sibling, before),
        (
            ("v", (2 * boxes * rank, double), BF16),
            ("v", (columns, boxes * rank), F32),
            ("v", coeffs.shape, BF16),
        ),
    )
    lists = (tile_target, tile_source, couple_offset, couple_class)
    gathered = held = coeffs
    after = send(own, lambda i: (i - 1) % count)
    for index, (low, wide) in enumerate(rounds_of(bits)):
        held = gathered
        kept = passed if index == 0 else gathered
        if index == 1:
            links = couple_offset.shape[1]
            maps, kept, places, targets, sources = call(
                functools.partial(map_kernel, bits),
                "maps",
                "shhhhhvvv" + "v" * steps,
                (device, *lists, list_coupling, gathered, transfer, sibling, *paths),
                (
                    ("v", ((count + links) * double, double), BF16),
                    ("v", gathered.shape, BF16),
                    ("v", (links, 8, 128), ints),
                    ("v", tile_target.shape, ints),
                    ("v", tile_source.shape, ints),
                ),
                scratch=(
                    pltpu.VMEM(couple_offset.shape, ints),
                    pltpu.VMEM(couple_class.shape, ints),
                    pltpu.VMEM(list_coupling.shape, F32),
                    dma((5,)),
                ),
            )
        parts = {0: kept}
        for step in range(2**wide - 1, 0, -1):
            parts[step] = swap(gathered, step << low)
        gathered = jnp.concatenate([parts[step] for step in range(2**wide)], axis=0)
    (near,) = call(
        near_kernel,
        "near",
        "sssvvvvv",
        (tile_count, targets, sources, before, own, after, near_tiles, held),
        (("v", (boxes, columns, points), F32),),
        scratch=(pltpu.VMEM((3 * boxes, columns, points), BF16),),
    )
    (field,) = call(
        field_kernel,
        "field",
        "vvvvvvv",
        (places, gathered, maps, spread, local, leaf_basis, near),
        (("v", (columns, width), F32),),
    )
    return field


def solution(mesh):
    in_specs = (
        P(None, AXES),
        P(AXES, None, None),
        P(),
        P(),
        P(),
        P(AXES, None, None),
        P(AXES),
        P(AXES),
        P(AXES),
        P(AXES, None),
        P(AXES, None),
    )
    return jax.shard_map(body, mesh=mesh, in_specs=in_specs, out_specs=P(None, AXES), check_vma=False)
```

```python
import functools

import jax
import jax.numpy as jnp
from jax import lax
from jax.experimental import pallas as pl
from jax.experimental.pallas import tpu as pltpu
from jax.sharding import PartitionSpec as P

AXES = ("leaf", "grp")
F32 = jnp.float32
BF16 = jnp.bfloat16
NN = (((1,), (0,)), ((), ()))
NT = (((1,), (1,)), ((), ()))
CHUNK = 512
STACK = 6 * 2**20


def split(x):
    high = x.astype(BF16)
    return high, (x - high.astype(F32)).astype(BF16)


def dot(a, b, dims=NN):
    return lax.dot_general(a, b, dims, preferred_element_type=F32)


def dot3(a, b, dims=NN):
    a_high, a_low = split(a)
    b_high, b_low = split(b)
    return dot(a_high, b_high, dims) + (dot(a_low, b_high, dims) + dot(a_high, b_low, dims))


def rounds_of(bits):
    rounds = []
    top = bits
    while top > 0:
        wide = 2 if top > 1 else 1
        rounds.append((top - wide, wide))
        top -= wide
    return rounds


def place_of(mask, bits):
    place, shift = 0, 0
    for low, wide in rounds_of(bits):
        place = place | ((-(mask >> low) & (2**wide - 1)) << shift)
        shift += wide
    return place


def up(blocks, transfer):
    left = jnp.concatenate(blocks[0::2], axis=0)
    right = jnp.concatenate(blocks[1::2], axis=0)
    rows = blocks[0].shape[0]
    total = dot3(left, transfer[0]) + dot3(right, transfer[1])
    return [total[i * rows : (i + 1) * rows] for i in range(len(blocks) // 2)]


def high_low(double):
    high, low = split(double)
    lane = lax.broadcasted_iota(jnp.int32, double.shape, 1)
    return jnp.where(lane < double.shape[1] // 2, high, low)


def twice(x):
    return jnp.concatenate([x, x], axis=1)


def both_halves(x):
    return x + pltpu.roll(x, x.shape[1] // 2, 1)


def start_copies(pairs, sems):
    copies = [pltpu.make_async_copy(a, b, sems.at[i]) for i, (a, b) in enumerate(pairs)]
    for copy in copies:
        copy.start()
    return copies


def leaf_kernel(transfer_hbm, vectors_hbm, sibling_hbm, basis_hbm, transfer, vectors, sibling, send, leaf, *refs):
    *paths, basis, sems = refs
    boxes, rank, points = basis.shape
    steps = boxes.bit_length() - 1
    pairs = ((transfer_hbm, transfer), (vectors_hbm, vectors), (basis_hbm, basis), (sibling_hbm, sibling))
    copies = start_copies(pairs, sems)
    copies[0].wait()
    t0, t1 = transfer[0], transfer[1]
    stack = jnp.concatenate([t0, t1], axis=0)
    for height in range(1, steps + 1):
        if height > 1:
            stack = jnp.concatenate([dot3(stack, t0), dot3(stack, t1)], axis=0)
        double = twice(stack)
        paths[height - 1][...] = double.reshape(paths[height - 1].shape)
    weights, rest = split(double)
    copies[1].wait()
    copies[2].wait()
    high, low = [], []
    for b in range(boxes):
        coeffs = dot(vectors[:, b * points : (b + 1) * points], basis[b], NT)
        leaf[b] = coeffs
        one, other = split(coeffs)
        high.append(one)
        low.append(other)
    high = jnp.concatenate(high, axis=1)
    low = jnp.concatenate(low, axis=1)
    send[0] = high_low(dot(high, weights) + (dot(low, weights) + dot(high, rest)))
    copies[3].wait()


def window_kernel(coeffs, before, own, window, passed):
    passed[...] = coeffs[...]
    boxes = window.shape[0] // 2
    points = window.shape[2]
    for i, part in enumerate((before, own)):
        for b in range(boxes):
            window[i * boxes + b] = part[:, b * points : (b + 1) * points]


def map_kernel(bits, device, *refs):
    hbm, (gathered, transfer, sibling), paths = refs[:5], refs[5:8], refs[8:-11]
    maps, rest, places, codes, passed, *here, sems = refs[-11:]
    copies = start_copies(zip(hbm, here), sems)
    _, _, offsets, classes, coupling = here
    rank = transfer.shape[1]
    passed[...] = gathered[...]
    me = device[0]
    side = me & 1
    pair = me >> 1
    count = 2**bits
    steps = len(paths)

    def put(table, at, double):
        both = high_low(double)
        if isinstance(at, int):
            at = at * 2 * rank
        else:
            at = pl.multiple_of(at * 2 * rank, 2 * rank)
        table[pl.ds(at, rank)] = both
        table[pl.ds(at + rank, rank)] = both

    def place(height, low):
        return place_of((1 << height) | (low ^ (pair & ((1 << height) - 1))), bits - 1)

    sides = []
    for height in range(1, steps + 1):
        tall = paths[height - 1][:, side].reshape(2 ** (height - 1) * rank, 2 * rank)
        sides.append(jnp.concatenate([high_low(tall), tall.astype(BF16)], axis=1))

    def climb(height, fan):
        fan_high, fan_low = split(fan)
        weights = jnp.concatenate([fan_high, fan_high, fan_low, jnp.zeros_like(fan_low)], axis=0)
        return dot(sides[height - 1], weights)

    t0, t1 = transfer[0], transfer[1]

    def path(height):
        if height <= steps:
            low = pair & ((1 << height) - 1)
            return paths[height - 1][low >> 1, low & 1][:, :rank]
        return dot3(path(height - 1), transfer[(pair >> (height - 1)) & 1])

    put(maps, 0, jnp.zeros((rank, 2 * rank), F32))
    wide = []
    for height in range(1, bits):
        bridge = sibling[(me >> height) & 1]
        if height > 1:
            bridge = dot3(bridge, path(height - 1), NT)
        fans = [twice(bridge)]
        for _ in range(height - steps):
            fans = [dot3(t, fan) for fan in fans for t in (t0, t1)]
        if height < steps:
            block = climb(height, fans[0])
            for i in range(2 ** (height - 1)):
                put(maps, place(height - 1, i), block[i * rank : (i + 1) * rank])
        else:
            wide += [(height, j, fan) for j, fan in enumerate(fans)]
    for start in range(0, len(wide), 4):
        part = wide[start : start + 4]
        block = climb(steps, jnp.concatenate([fan for _, _, fan in part], axis=1))
        for k, (height, j, _) in enumerate(part):
            for i in range(2 ** (steps - 1)):
                one = block[i * rank : (i + 1) * rank, k * 2 * rank : (k + 1) * 2 * rank]
                put(maps, place(height - 1, (j << (steps - 1)) + i), one)
    put(rest, 0, twice(sibling[side]))
    for copy in copies:
        copy.wait()
    lane = lax.broadcasted_iota(jnp.int32, offsets.shape, 1)
    for i in range(offsets.shape[1]):
        offset = jnp.sum(jnp.where(lane == i, offsets[...], 0))
        kind = jnp.sum(jnp.where(lane == i, classes[...], 0))
        mask = ((me + offset + count) & (count - 1)) ^ me
        here_too = (mask & 1) == 0
        link = jnp.where(here_too, place_of(mask >> 1, bits - 1), 0)
        places[i] = jnp.full(places.shape[1:], link, jnp.int32)
        code = jnp.where(here_too, 0, jnp.where(mask == 1, 1, 2))
        codes[i] = jnp.full(codes.shape[1:], code, jnp.int32)
        put(rest, 1 + i, twice(coupling[kind]))


def near_kernel(live, targets, sources, window, after, tiles, blocks, gathered, places, near, links, right):
    for i in range(links.shape[0]):
        links[i] = gathered[jnp.max(places[i])]
    slots, points, _ = tiles.shape
    boxes = near.shape[0]
    for b in range(boxes):
        right[b] = after[:, b * points : (b + 1) * points]
    near[...] = jnp.zeros_like(near)
    for slot in range(slots):
        box = sources[slot]
        inner = window[jnp.minimum(box, 2 * boxes - 1)]
        outer = right[jnp.maximum(box - 2 * boxes, 0)]
        source = jnp.where(box < 2 * boxes, inner, outer)
        source = jnp.where(slot < live[0], source, jnp.zeros_like(source))
        target = targets[slot]
        near[target] = near[target] + dot(source, tiles[slot])


def half_kernel(bits, device, gathered, maps, send, total):
    count = gathered.shape[0]
    wide = 2 * maps.shape[1]
    me = device[0]

    def step(k):
        coeffs = jnp.concatenate([gathered[2 * k], gathered[2 * k + 1]], axis=1)
        return dot(coeffs, maps[pl.ds(k * wide, wide)])

    pairs = count // 2
    if pairs <= 32:
        both = step(0)
        for k in range(1, pairs):
            both = both + step(k)
    else:
        both = lax.fori_loop(1, pairs, lambda k, sums: sums + step(k), step(0))
    sums = both_halves(both)
    total[...] = sums
    across = me + jnp.where((me & 1) == 1, -2, 2)
    mask = (across & (2**bits - 1)) ^ me
    send[0] = gathered[0]
    send[1] = gathered[place_of(mask >> 1, bits - 1)]
    send[2] = high_low(sums)


def down_kernel(device, leaf, paths, transfer, sibling, gathered, spread, local, passed):
    boxes, columns, rank = leaf.shape
    half = boxes * rank
    passed[...] = gathered[...]
    t0, t1 = transfer[0], transfer[1]
    s0, s1 = sibling[0], sibling[1]
    tall = paths[...].reshape(half, 2 * rank)
    high, low = split(tall)
    spread[:half, 2 * rank :] = high
    spread[half:, 2 * rank :] = low
    mine_high, mine_low = split(twice(transfer[device[0] & 1]))
    weights = jnp.concatenate([mine_high, mine_high, mine_low, jnp.zeros_like(mine_low)], axis=0)
    high, low = split(dot(jnp.concatenate([high_low(tall), high], axis=1), weights))
    spread[:half, : 2 * rank] = high
    spread[half:, : 2 * rank] = low
    levels = [[leaf[b] for b in range(boxes)]]
    while len(levels[-1]) > 2:
        levels.append(up(levels[-1], (t0, t1)))
    down = None
    for level in reversed(levels):
        across0 = dot3(jnp.concatenate(level[1::2], axis=0), s0)
        across1 = dot3(jnp.concatenate(level[0::2], axis=0), s1)
        if down is not None:
            parents = jnp.concatenate(down, axis=0)
            across0 = across0 + dot3(parents, t0, NT)
            across1 = across1 + dot3(parents, t1, NT)
        down = []
        for i in range(len(level) // 2):
            down.append(across0[i * columns : (i + 1) * columns])
            down.append(across1[i * columns : (i + 1) * columns])
    for b in range(boxes):
        local[:, b * rank : (b + 1) * rank] = down[b]


def field_kernel(other, links, codes, rest, total, spread, local, basis, near, field):
    boxes, rank, points = basis.shape
    parts = [other[0]]
    for i in range(links.shape[0]):
        code = codes[i]
        elsewhere = jnp.where(code == 1, other[0].astype(F32), other[1].astype(F32))
        parts.append(jnp.where(code == 0, links[i].astype(F32), elsewhere).astype(BF16))
    mine = both_halves(dot(jnp.concatenate(parts, axis=1), rest[...]))
    pair = total[...] + both_halves(other[2].astype(F32))
    doubled = dot(jnp.concatenate([high_low(pair), high_low(mine)], axis=1), spread[...], NT)
    half = boxes * rank
    rounded = (doubled[:, :half] + doubled[:, half:] + local[...]).astype(BF16)
    for b in range(boxes):
        far = dot(rounded[:, b * rank : (b + 1) * rank], basis[b])
        field[:, b * points : (b + 1) * points] = near[b] + far


SPACES = {"v": pltpu.VMEM, "s": pltpu.SMEM, "h": pl.ANY}


def call(kernel, name, kinds, args, outs, scratch=(), flops=0):
    moved = sum(x.size * x.dtype.itemsize for x in args)
    held = [x for x, kind in zip(args, kinds) if kind == "v"]
    held += [jax.ShapeDtypeStruct(shape, kind) for space, shape, kind in outs if space == "v"]
    limit = STACK + sum(x.size // x.shape[-1] * max(x.shape[-1], 128) * x.dtype.itemsize for x in held)
    args = [
        pltpu.with_memory_space_constraint(x, pltpu.HBM) if kind == "h" else x
        for kind, x in zip(kinds, args)
    ]
    return pl.pallas_call(
        kernel,
        name=name,
        out_shape=[jax.ShapeDtypeStruct(shape, kind) for _, shape, kind in outs],
        in_specs=[pl.BlockSpec(memory_space=SPACES[kind]) for kind in kinds],
        out_specs=[pl.BlockSpec(memory_space=SPACES[space]) for space, _, _ in outs],
        scratch_shapes=list(scratch),
        compiler_params=pltpu.CompilerParams(vmem_limit_bytes=limit),
        cost_estimate=pl.CostEstimate(flops=flops, bytes_accessed=moved, transcendentals=0),
    )(*args)


def body(
    vectors,
    leaf_basis,
    transfer,
    sibling_coupling,
    list_coupling,
    near_tiles,
    tile_target,
    tile_source,
    tile_count,
    couple_offset,
    couple_class,
):
    columns, width = vectors.shape
    boxes, rank, points = leaf_basis.shape
    count = lax.axis_size(AXES)
    bits = count.bit_length() - 1
    steps = boxes.bit_length() - 1
    double = 2 * rank
    dma = pltpu.SemaphoreType.DMA

    def send(x, target):
        return lax.ppermute(x, AXES, [(i, target(i)) for i in range(count)])

    def swap(x, mask):
        return send(x, lambda i: i ^ mask)

    before = send(vectors, lambda i: (i + 1) % count)
    ints = jnp.int32
    plain = (transfer, vectors, sibling_coupling)
    path_shapes = [(2 ** (height - 1), 2, rank, double) for height in range(1, steps + 1)]
    transfer, own, sibling, coeffs, leaf, *paths = call(
        leaf_kernel,
        "leaf",
        "hhhh",
        (*plain, leaf_basis),
        (
            *(("v", x.shape, x.dtype) for x in plain),
            ("v", (1, columns, double), BF16),
            ("v", (boxes, columns, rank), F32),
            *(("v", shape, F32) for shape in path_shapes),
        ),
        scratch=(pltpu.VMEM(leaf_basis.shape, BF16), dma((4,))),
    )
    device = lax.axis_index(AXES).astype(ints).reshape(1)
    window, passed = call(
        window_kernel,
        "window",
        "vvv",
        (coeffs, before, own),
        (("v", (2 * boxes, columns, points), BF16), ("v", coeffs.shape, BF16)),
    )
    lists = (tile_target, tile_source, couple_offset, couple_class)
    links = couple_offset.shape[1]
    gathered = coeffs
    after = send(own, lambda i: (i - 1) % count)
    for index, (low, wide) in enumerate(rounds_of(bits - 1)):
        kept = passed if index == 0 else gathered
        if index == 1:
            maps, rest, places, codes, kept, targets, sources = call(
                functools.partial(map_kernel, bits),
                "maps",
                "shhhhhvvv" + "v" * steps,
                (device, *lists, list_coupling, gathered, transfer, sibling, *paths),
                (
                    ("v", (count // 2 * double, double), BF16),
                    ("v", ((1 + links) * double, double), BF16),
                    ("v", (links, 8, 128), ints),
                    ("v", (links, columns, double), ints),
                    ("v", gathered.shape, BF16),
                    ("v", tile_target.shape, ints),
                    ("v", tile_source.shape, ints),
                ),
                scratch=(
                    pltpu.VMEM(couple_offset.shape, ints),
                    pltpu.VMEM(couple_class.shape, ints),
                    pltpu.VMEM(list_coupling.shape, F32),
                    dma((5,)),
                ),
            )
            spread, local, kept = call(
                down_kernel,
                "down",
                "svvvvv",
                (device, leaf, paths[-1], transfer, sibling, kept),
                (
                    ("v", (2 * boxes * rank, 2 * double), BF16),
                    ("v", (columns, boxes * rank), F32),
                    ("v", gathered.shape, BF16),
                ),
            )
        parts = {0: kept}
        for step in range(2**wide - 1, 0, -1):
            parts[step] = swap(gathered, 2 * step << low)
        gathered = jnp.concatenate([parts[-step % 2**wide] for step in range(2**wide)], axis=0)
    blocks, total = call(
        functools.partial(half_kernel, bits),
        "half",
        "svv",
        (device, gathered, maps),
        (("v", (3, columns, double), BF16), ("v", (columns, double), F32)),
    )
    other = swap(blocks, 1)
    near, picked = call(
        near_kernel,
        "near",
        "sssvvvvvv",
        (tile_count, targets, sources, window, after, near_tiles, blocks, gathered, places),
        (("v", (boxes, columns, points), F32), ("v", (links, columns, double), BF16)),
        scratch=(pltpu.VMEM((boxes, columns, points), BF16),),
    )
    (field,) = call(
        field_kernel,
        "field",
        "v" * 9,
        (other, picked, codes, rest, total, spread, local, leaf_basis, near),
        (("v", (columns, width), F32),),
    )
    return field


def solution(mesh):
    in_specs = (
        P(None, AXES),
        P(AXES, None, None),
        P(),
        P(),
        P(),
        P(AXES, None, None),
        P(AXES),
        P(AXES),
        P(AXES),
        P(AXES, None),
        P(AXES, None),
    )
    return jax.shard_map(body, mesh=mesh, in_specs=in_specs, out_specs=P(None, AXES), check_vma=False)
```

```python
import functools

import jax
import jax.numpy as jnp
from jax import lax
from jax.experimental import pallas as pl
from jax.experimental.pallas import tpu as pltpu
from jax.sharding import PartitionSpec as P

AXES = ("leaf", "grp")
F32 = jnp.float32
BF16 = jnp.bfloat16
NN = (((1,), (0,)), ((), ()))
NT = (((1,), (1,)), ((), ()))
CHUNK = 512
STACK = 6 * 2**20


def split(x):
    high = x.astype(BF16)
    return high, (x - high.astype(F32)).astype(BF16)


def dot(a, b, dims=NN):
    return lax.dot_general(a, b, dims, preferred_element_type=F32)


def dot3(a, b, dims=NN):
    a_high, a_low = split(a)
    b_high, b_low = split(b)
    return dot(a_high, b_high, dims) + (dot(a_low, b_high, dims) + dot(a_high, b_low, dims))


def rounds_of(bits):
    rounds = []
    top = bits
    while top > 0:
        wide = 2 if top > 1 else 1
        rounds.append((top - wide, wide))
        top -= wide
    return rounds


def place_of(source, here, bits):
    place, shift = 0, 0
    for low, wide in rounds_of(bits):
        place = place | ((((here >> low) - (source >> low)) & (2**wide - 1)) << shift)
        shift += wide
    return place


def up(blocks, transfer):
    left = jnp.concatenate(blocks[0::2], axis=0)
    right = jnp.concatenate(blocks[1::2], axis=0)
    rows = blocks[0].shape[0]
    total = dot3(left, transfer[0]) + dot3(right, transfer[1])
    return [total[i * rows : (i + 1) * rows] for i in range(len(blocks) // 2)]


def high_low(double):
    high, low = split(double)
    lane = lax.broadcasted_iota(jnp.int32, double.shape, 1)
    return jnp.where(lane < double.shape[1] // 2, high, low)


def twice(x):
    return jnp.concatenate([x, x], axis=1)


def both_halves(x):
    return x + pltpu.roll(x, x.shape[1] // 2, 1)


def packed(double):
    high, low = split(double)
    lane = lax.broadcasted_iota(jnp.int32, double.shape, 1)
    return jnp.concatenate([jnp.where(lane < double.shape[1] // 2, high, low), high], axis=1)


def packing(right):
    high, low = split(right)
    return jnp.concatenate([high, high, low, jnp.zeros_like(low)], axis=0)


def start_copies(pairs, sems):
    copies = [pltpu.make_async_copy(a, b, sems.at[i]) for i, (a, b) in enumerate(pairs)]
    for copy in copies:
        copy.start()
    return copies


def leaf_kernel(transfer_hbm, vectors_hbm, sibling_hbm, basis_hbm, transfer, vectors, sibling, send, leaf, *refs):
    *paths, basis, sems = refs
    boxes, rank, points = basis.shape
    steps = boxes.bit_length() - 1
    pairs = ((transfer_hbm, transfer), (vectors_hbm, vectors), (basis_hbm, basis), (sibling_hbm, sibling))
    copies = start_copies(pairs, sems)
    copies[0].wait()
    t0, t1 = twice(transfer[0]), twice(transfer[1])
    double = jnp.concatenate([t0, t1], axis=0)
    sides = packing(jnp.concatenate([t0, t1], axis=1))
    for height in range(1, steps + 1):
        if height > 1:
            wide = dot(packed(double), sides)
            double = jnp.concatenate([wide[:, : 2 * rank], wide[:, 2 * rank :]], axis=0)
        paths[height - 1][...] = double.reshape(paths[height - 1].shape)
    weights = jnp.concatenate(split(double), axis=1)
    copies[1].wait()
    copies[2].wait()
    high, low = [], []
    for b in range(boxes):
        coeffs = dot(vectors[:, b * points : (b + 1) * points], basis[b], NT)
        leaf[b] = coeffs
        one, other = split(coeffs)
        high.append(one)
        low.append(other)
    high = jnp.concatenate(high, axis=1)
    low = jnp.concatenate(low, axis=1)
    sums = dot(high, weights)
    sums = sums[:, : 2 * rank] + (sums[:, 2 * rank :] + dot(low, weights[:, : 2 * rank]))
    send[0] = high_low(sums)
    copies[3].wait()


def window_kernel(coeffs, before, own, window, passed):
    passed[...] = coeffs[...]
    boxes = window.shape[0] // 2
    points = window.shape[2]
    for i, part in enumerate((before, own)):
        for b in range(boxes):
            window[i * boxes + b] = part[:, b * points : (b + 1) * points]


def fill_down(me, leaf, paths, transfer, sibling, spread, local):
    boxes, columns, rank = leaf.shape
    half = boxes * rank
    t0, t1 = transfer[0], transfer[1]
    s0, s1 = sibling[0], sibling[1]
    tall = paths[...].reshape(half, 2 * rank)
    high, low = split(tall)
    spread[:half, 2 * rank :] = high
    spread[half:, 2 * rank :] = low
    high, low = split(dot(packed(tall), packing(twice(transfer[me & 1]))))
    spread[:half, : 2 * rank] = high
    spread[half:, : 2 * rank] = low
    levels = [[leaf[b] for b in range(boxes)]]
    while len(levels[-1]) > 2:
        levels.append(up(levels[-1], (t0, t1)))
    down = None
    for level in reversed(levels):
        across0 = dot3(jnp.concatenate(level[1::2], axis=0), s0)
        across1 = dot3(jnp.concatenate(level[0::2], axis=0), s1)
        if down is not None:
            parents = jnp.concatenate(down, axis=0)
            across0 = across0 + dot3(parents, t0, NT)
            across1 = across1 + dot3(parents, t1, NT)
        down = []
        for i in range(len(level) // 2):
            down.append(across0[i * columns : (i + 1) * columns])
            down.append(across1[i * columns : (i + 1) * columns])
    for b in range(boxes):
        local[:, b * rank : (b + 1) * rank] = down[b]


def map_kernel(bits, device, *refs):
    hbm, (gathered, transfer, sibling, leaf), paths = refs[:5], refs[5:9], refs[9:-13]
    maps, rest, places, codes, passed, spread, local, *here, sems = refs[-13:]
    copies = start_copies(zip(hbm, here), sems)
    _, _, offsets, classes, coupling = here
    rank = transfer.shape[1]
    passed[...] = gathered[...]
    me = device[0]
    side = me & 1
    pair = me >> 1
    count = 2**bits
    steps = len(paths)

    def put(table, at, double):
        both = high_low(double)
        if isinstance(at, int):
            at = at * 2 * rank
        else:
            at = pl.multiple_of(at * 2 * rank, 2 * rank)
        table[pl.ds(at, rank)] = both
        table[pl.ds(at + rank, rank)] = both

    def place(height, low):
        return place_of((((pair >> height) ^ 1) << height) | low, pair, bits - 1)

    sides = []
    for height in range(1, steps + 1):
        tall = paths[height - 1][:, side].reshape(2 ** (height - 1) * rank, 2 * rank)
        sides.append(packed(tall))

    def climb(height, fan):
        return dot(sides[height - 1], packing(fan))

    t0, t1 = transfer[0], transfer[1]

    def path(height):
        if height <= steps:
            low = pair & ((1 << height) - 1)
            return paths[height - 1][low >> 1, low & 1][:, :rank]
        return dot3(path(height - 1), transfer[(pair >> (height - 1)) & 1])

    put(maps, 0, jnp.zeros((rank, 2 * rank), F32))
    wide = []
    for height in range(1, bits):
        bridge = sibling[(me >> height) & 1]
        if height > 1:
            bridge = dot3(bridge, path(height - 1), NT)
        fans = [twice(bridge)]
        for _ in range(height - steps):
            fans = [dot3(t, fan) for fan in fans for t in (t0, t1)]
        if height < steps:
            block = climb(height, fans[0])
            for i in range(2 ** (height - 1)):
                put(maps, place(height - 1, i), block[i * rank : (i + 1) * rank])
        else:
            wide += [(height, j, fan) for j, fan in enumerate(fans)]
    for start in range(0, len(wide), 4):
        part = wide[start : start + 4]
        block = climb(steps, jnp.concatenate([fan for _, _, fan in part], axis=1))
        for k, (height, j, _) in enumerate(part):
            for i in range(2 ** (steps - 1)):
                one = block[i * rank : (i + 1) * rank, k * 2 * rank : (k + 1) * 2 * rank]
                put(maps, place(height - 1, (j << (steps - 1)) + i), one)
    put(rest, 0, twice(sibling[side]))
    fill_down(me, leaf, paths[-1], transfer, sibling, spread, local)
    for copy in copies:
        copy.wait()
    for i in range(offsets.shape[1]):
        offset = offsets[0, i]
        kind = classes[0, i]
        source = (me + offset + count) & (count - 1)
        here_too = ((source ^ me) & 1) == 0
        link = jnp.where(here_too, place_of(source >> 1, pair, bits - 1), 0)
        places[i] = jnp.full(places.shape[1:], link, jnp.int32)
        code = jnp.where(here_too, 0, jnp.where(source == me ^ 1, 1, 2))
        codes[i] = jnp.full(codes.shape[1:], code, jnp.int32)
        put(rest, 1 + i, twice(coupling[kind]))


def near_kernel(live, targets, sources, window, after, tiles, blocks, gathered, places, near, links, right):
    for i in range(links.shape[0]):
        links[i] = gathered[jnp.max(places[i])]
    slots, points, _ = tiles.shape
    boxes = near.shape[0]
    for b in range(boxes):
        right[b] = after[:, b * points : (b + 1) * points]
    near[...] = jnp.zeros_like(near)
    for slot in range(slots):
        box = sources[slot]
        inner = window[jnp.minimum(box, 2 * boxes - 1)]
        outer = right[jnp.maximum(box - 2 * boxes, 0)]
        source = jnp.where(box < 2 * boxes, inner, outer)
        source = jnp.where(slot < live[0], source, jnp.zeros_like(source))
        target = targets[slot]
        near[target] = near[target] + dot(source, tiles[slot])


def half_kernel(bits, device, gathered, maps, send, total):
    count = gathered.shape[0]
    wide = 2 * maps.shape[1]
    me = device[0]

    def step(k):
        coeffs = jnp.concatenate([gathered[2 * k], gathered[2 * k + 1]], axis=1)
        return dot(coeffs, maps[pl.ds(k * wide, wide)])

    pairs = count // 2
    if pairs <= 32:
        both = step(0)
        for k in range(1, pairs):
            both = both + step(k)
    else:
        both = lax.fori_loop(1, pairs, lambda k, sums: sums + step(k), step(0))
    sums = both_halves(both)
    total[...] = sums
    across = (me + jnp.where((me & 1) == 1, -2, 2)) & (2**bits - 1)
    send[0] = gathered[0]
    send[1] = gathered[place_of(across >> 1, me >> 1, bits - 1)]
    send[2] = high_low(sums)


def field_kernel(other, links, codes, rest, total, spread, local, basis, near, field):
    boxes, rank, points = basis.shape
    parts = [other[0]]
    for i in range(links.shape[0]):
        code = codes[i]
        elsewhere = jnp.where(code == 1, other[0].astype(F32), other[1].astype(F32))
        parts.append(jnp.where(code == 0, links[i].astype(F32), elsewhere).astype(BF16))
    mine = both_halves(dot(jnp.concatenate(parts, axis=1), rest[...]))
    pair = total[...] + both_halves(other[2].astype(F32))
    doubled = dot(jnp.concatenate([high_low(pair), high_low(mine)], axis=1), spread[...], NT)
    half = boxes * rank
    rounded = (doubled[:, :half] + doubled[:, half:] + local[...]).astype(BF16)
    for b in range(boxes):
        far = dot(rounded[:, b * rank : (b + 1) * rank], basis[b])
        field[:, b * points : (b + 1) * points] = near[b] + far


SPACES = {"v": pltpu.VMEM, "s": pltpu.SMEM, "h": pl.ANY}


def call(kernel, name, kinds, args, outs, scratch=(), flops=0):
    moved = sum(x.size * x.dtype.itemsize for x in args)
    held = [x for x, kind in zip(args, kinds) if kind == "v"]
    held += [jax.ShapeDtypeStruct(shape, kind) for space, shape, kind in outs if space == "v"]
    limit = STACK + sum(x.size // x.shape[-1] * max(x.shape[-1], 128) * x.dtype.itemsize for x in held)
    args = [
        pltpu.with_memory_space_constraint(x, pltpu.HBM) if kind == "h" else x
        for kind, x in zip(kinds, args)
    ]
    return pl.pallas_call(
        kernel,
        name=name,
        out_shape=[jax.ShapeDtypeStruct(shape, kind) for _, shape, kind in outs],
        in_specs=[pl.BlockSpec(memory_space=SPACES[kind]) for kind in kinds],
        out_specs=[pl.BlockSpec(memory_space=SPACES[space]) for space, _, _ in outs],
        scratch_shapes=list(scratch),
        compiler_params=pltpu.CompilerParams(vmem_limit_bytes=limit),
        cost_estimate=pl.CostEstimate(flops=flops, bytes_accessed=moved, transcendentals=0),
    )(*args)


def body(
    vectors,
    leaf_basis,
    transfer,
    sibling_coupling,
    list_coupling,
    near_tiles,
    tile_target,
    tile_source,
    tile_count,
    couple_offset,
    couple_class,
):
    columns, width = vectors.shape
    boxes, rank, points = leaf_basis.shape
    count = lax.axis_size(AXES)
    bits = count.bit_length() - 1
    steps = boxes.bit_length() - 1
    double = 2 * rank
    dma = pltpu.SemaphoreType.DMA

    def send(x, target):
        return lax.ppermute(x, AXES, [(i, target(i)) for i in range(count)])

    def turned(i, low, wide, step):
        digit = (i >> low) % 2**wide
        return i + (((digit + step) % 2**wide - digit) << low)

    before = send(vectors, lambda i: (i + 1) % count)
    ints = jnp.int32
    plain = (transfer, vectors, sibling_coupling)
    path_shapes = [(2 ** (height - 1), 2, rank, double) for height in range(1, steps + 1)]
    transfer, own, sibling, coeffs, leaf, *paths = call(
        leaf_kernel,
        "leaf",
        "hhhh",
        (*plain, leaf_basis),
        (
            *(("v", x.shape, x.dtype) for x in plain),
            ("v", (1, columns, double), BF16),
            ("v", (boxes, columns, rank), F32),
            *(("v", shape, F32) for shape in path_shapes),
        ),
        scratch=(pltpu.VMEM(leaf_basis.shape, BF16), dma((4,))),
    )
    device = lax.axis_index(AXES).astype(ints).reshape(1)
    window, passed = call(
        window_kernel,
        "window",
        "vvv",
        (coeffs, before, own),
        (("v", (2 * boxes, columns, points), BF16), ("v", coeffs.shape, BF16)),
    )
    lists = (tile_target, tile_source, couple_offset, couple_class)
    links = couple_offset.shape[1]
    gathered = coeffs
    after = send(own, lambda i: (i - 1) % count)
    for index, (low, wide) in enumerate(rounds_of(bits - 1)):
        kept = passed if index == 0 else gathered
        if index == 1:
            maps, rest, places, codes, kept, spread, local, targets, sources = call(
                functools.partial(map_kernel, bits),
                "maps",
                "shhhhhvvvv" + "v" * steps,
                (device, *lists, list_coupling, gathered, transfer, sibling, leaf, *paths),
                (
                    ("v", (count // 2 * double, double), BF16),
                    ("v", ((1 + links) * double, double), BF16),
                    ("v", (links, 8, 128), ints),
                    ("v", (links, columns, double), ints),
                    ("v", gathered.shape, BF16),
                    ("v", (2 * boxes * rank, 2 * double), BF16),
                    ("v", (columns, boxes * rank), F32),
                    ("v", tile_target.shape, ints),
                    ("v", tile_source.shape, ints),
                ),
                scratch=(
                    pltpu.SMEM(couple_offset.shape, ints),
                    pltpu.SMEM(couple_class.shape, ints),
                    pltpu.VMEM(list_coupling.shape, F32),
                    dma((5,)),
                ),
            )
        parts = [kept]
        for step in range(1, 2**wide):
            parts.append(send(gathered, lambda i, args=(low + 1, wide, step): turned(i, *args)))
        gathered = jnp.concatenate(parts, axis=0)
    blocks, total = call(
        functools.partial(half_kernel, bits),
        "half",
        "svv",
        (device, gathered, maps),
        (("v", (3, columns, double), BF16), ("v", (columns, double), F32)),
    )
    other = send(blocks, lambda i: i ^ 1)
    near, picked = call(
        near_kernel,
        "near",
        "sssvvvvvv",
        (tile_count, targets, sources, window, after, near_tiles, blocks, gathered, places),
        (("v", (boxes, columns, points), F32), ("v", (links, columns, double), BF16)),
        scratch=(pltpu.VMEM((boxes, columns, points), BF16),),
    )
    (field,) = call(
        field_kernel,
        "field",
        "v" * 9,
        (other, picked, codes, rest, total, spread, local, leaf_basis, near),
        (("v", (columns, width), F32),),
    )
    return field


def solution(mesh):
    in_specs = (
        P(None, AXES),
        P(AXES, None, None),
        P(),
        P(),
        P(),
        P(AXES, None, None),
        P(AXES),
        P(AXES),
        P(AXES),
        P(AXES, None),
        P(AXES, None),
    )
    return jax.shard_map(body, mesh=mesh, in_specs=in_specs, out_specs=P(None, AXES), check_vma=False)
```

```python
import functools

import jax
import jax.numpy as jnp
from jax import lax
from jax.experimental import pallas as pl
from jax.experimental.pallas import tpu as pltpu
from jax.sharding import PartitionSpec as P

AXES = ("leaf", "grp")
F32 = jnp.float32
BF16 = jnp.bfloat16
NN = (((1,), (0,)), ((), ()))
NT = (((1,), (1,)), ((), ()))
CHUNK = 512
STACK = 6 * 2**20


def split(x):
    high = x.astype(BF16)
    return high, (x - high.astype(F32)).astype(BF16)


def dot(a, b, dims=NN):
    return lax.dot_general(a, b, dims, preferred_element_type=F32)


def dot3(a, b, dims=NN):
    a_high, a_low = split(a)
    b_high, b_low = split(b)
    return dot(a_high, b_high, dims) + (dot(a_low, b_high, dims) + dot(a_high, b_low, dims))


def rounds_of(bits):
    rounds = []
    top = bits
    while top > 0:
        wide = 2 if top > 1 else 1
        rounds.append((top - wide, wide))
        top -= wide
    return rounds


def place_of(source, here, bits):
    place, shift = 0, 0
    for low, wide in rounds_of(bits):
        place = place | ((((here >> low) - (source >> low)) & (2**wide - 1)) << shift)
        shift += wide
    return place


def up(blocks, transfer):
    left = jnp.concatenate(blocks[0::2], axis=0)
    right = jnp.concatenate(blocks[1::2], axis=0)
    rows = blocks[0].shape[0]
    total = dot3(left, transfer[0]) + dot3(right, transfer[1])
    return [total[i * rows : (i + 1) * rows] for i in range(len(blocks) // 2)]


def high_low(double):
    high, low = split(double)
    lane = lax.broadcasted_iota(jnp.int32, double.shape, 1)
    return jnp.where(lane < double.shape[1] // 2, high, low)


def twice(x):
    return jnp.concatenate([x, x], axis=1)


def both_halves(x):
    return x + pltpu.roll(x, x.shape[1] // 2, 1)


def packed(double):
    high, low = split(double)
    lane = lax.broadcasted_iota(jnp.int32, double.shape, 1)
    return jnp.concatenate([jnp.where(lane < double.shape[1] // 2, high, low), high], axis=1)


def packing(right):
    high, low = split(right)
    return jnp.concatenate([high, high, low, jnp.zeros_like(low)], axis=0)


def start_copies(pairs, sems):
    copies = [pltpu.make_async_copy(a, b, sems.at[i]) for i, (a, b) in enumerate(pairs)]
    for copy in copies:
        copy.start()
    return copies


def leaf_kernel(transfer_hbm, vectors_hbm, sibling_hbm, basis_hbm, transfer, vectors, sibling, send, leaf, *refs):
    *paths, basis, sems = refs
    boxes, rank, points = basis.shape
    steps = boxes.bit_length() - 1
    pairs = ((transfer_hbm, transfer), (vectors_hbm, vectors), (basis_hbm, basis), (sibling_hbm, sibling))
    copies = start_copies(pairs, sems)
    copies[0].wait()
    t0, t1 = twice(transfer[0]), twice(transfer[1])
    double = jnp.concatenate([t0, t1], axis=0)
    sides = packing(jnp.concatenate([t0, t1], axis=1))
    for height in range(1, steps + 1):
        if height == steps:
            copies[1].wait()
            copies[2].wait()
            high, low = [], []
            for b in range(boxes):
                coeffs = dot(vectors[:, b * points : (b + 1) * points], basis[b], NT)
                leaf[b] = coeffs
                one, other = split(coeffs)
                high.append(one)
                low.append(other)
        if height > 1:
            wide = dot(packed(double), sides)
            double = jnp.concatenate([wide[:, : 2 * rank], wide[:, 2 * rank :]], axis=0)
        paths[height - 1][...] = double.reshape(paths[height - 1].shape)
    weights = jnp.concatenate(split(double), axis=1)
    high = jnp.concatenate(high, axis=1)
    low = jnp.concatenate(low, axis=1)
    sums = dot(high, weights)
    sums = sums[:, : 2 * rank] + (sums[:, 2 * rank :] + dot(low, weights[:, : 2 * rank]))
    send[0] = high_low(sums)
    copies[3].wait()


def window_kernel(coeffs, before, own, window, passed):
    passed[...] = coeffs[...]
    boxes = window.shape[0] // 2
    points = window.shape[2]
    for i, part in enumerate((before, own)):
        for b in range(boxes):
            window[i * boxes + b] = part[:, b * points : (b + 1) * points]


def fill_down(me, leaf, paths, transfer, sibling, spread, local):
    boxes, columns, rank = leaf.shape
    half = boxes * rank
    t0, t1 = transfer[0], transfer[1]
    s0, s1 = sibling[0], sibling[1]
    tall = paths[...].reshape(half, 2 * rank)
    high, low = split(tall)
    spread[:half, 2 * rank :] = high
    spread[half:, 2 * rank :] = low
    high, low = split(dot(packed(tall), packing(twice(transfer[me & 1]))))
    spread[:half, : 2 * rank] = high
    spread[half:, : 2 * rank] = low
    levels = [[leaf[b] for b in range(boxes)]]
    while len(levels[-1]) > 2:
        levels.append(up(levels[-1], (t0, t1)))
    down = None
    for level in reversed(levels):
        across0 = dot3(jnp.concatenate(level[1::2], axis=0), s0)
        across1 = dot3(jnp.concatenate(level[0::2], axis=0), s1)
        if down is not None:
            parents = jnp.concatenate(down, axis=0)
            across0 = across0 + dot3(parents, t0, NT)
            across1 = across1 + dot3(parents, t1, NT)
        down = []
        for i in range(len(level) // 2):
            down.append(across0[i * columns : (i + 1) * columns])
            down.append(across1[i * columns : (i + 1) * columns])
    for b in range(boxes):
        local[:, b * rank : (b + 1) * rank] = down[b]


def map_kernel(bits, device, *refs):
    hbm, (gathered, transfer, sibling, leaf), paths = refs[:5], refs[5:9], refs[9:-13]
    maps, rest, places, codes, passed, spread, local, *here, sems = refs[-13:]
    copies = start_copies(zip(hbm, here), sems)
    _, _, offsets, classes, coupling = here
    rank = transfer.shape[1]
    passed[...] = gathered[...]
    me = device[0]
    side = me & 1
    pair = me >> 1
    count = 2**bits
    steps = len(paths)

    def put(table, at, double):
        both = high_low(double)
        if isinstance(at, int):
            at = at * 2 * rank
        else:
            at = pl.multiple_of(at * 2 * rank, 2 * rank)
        table[pl.ds(at, rank)] = both
        table[pl.ds(at + rank, rank)] = both

    def place(height, low):
        return place_of((((pair >> height) ^ 1) << height) | low, pair, bits - 1)

    sides = []
    for height in range(1, steps + 1):
        tall = paths[height - 1][:, side].reshape(2 ** (height - 1) * rank, 2 * rank)
        sides.append(packed(tall))

    def climb(height, fan):
        return dot(sides[height - 1], packing(fan))

    t0, t1 = transfer[0], transfer[1]

    def path(height):
        if height <= steps:
            low = pair & ((1 << height) - 1)
            return paths[height - 1][low >> 1, low & 1][:, :rank]
        return dot3(path(height - 1), transfer[(pair >> (height - 1)) & 1])

    put(maps, 0, jnp.zeros((rank, 2 * rank), F32))
    wide = []
    for height in range(1, bits):
        bridge = sibling[(me >> height) & 1]
        if height > 1:
            bridge = dot3(bridge, path(height - 1), NT)
        fans = [twice(bridge)]
        for _ in range(height - steps):
            fans = [dot3(t, fan) for fan in fans for t in (t0, t1)]
        if height < steps:
            block = climb(height, fans[0])
            for i in range(2 ** (height - 1)):
                put(maps, place(height - 1, i), block[i * rank : (i + 1) * rank])
        else:
            wide += [(height, j, fan) for j, fan in enumerate(fans)]
    for start in range(0, len(wide), 4):
        part = wide[start : start + 4]
        block = climb(steps, jnp.concatenate([fan for _, _, fan in part], axis=1))
        for k, (height, j, _) in enumerate(part):
            for i in range(2 ** (steps - 1)):
                one = block[i * rank : (i + 1) * rank, k * 2 * rank : (k + 1) * 2 * rank]
                put(maps, place(height - 1, (j << (steps - 1)) + i), one)
    put(rest, 0, twice(sibling[side]))
    fill_down(me, leaf, paths[-1], transfer, sibling, spread, local)
    for copy in copies:
        copy.wait()
    for i in range(offsets.shape[1]):
        offset = offsets[0, i]
        kind = classes[0, i]
        source = (me + offset + count) & (count - 1)
        here_too = ((source ^ me) & 1) == 0
        link = jnp.where(here_too, place_of(source >> 1, pair, bits - 1), 0)
        places[i] = jnp.full(places.shape[1:], link, jnp.int32)
        code = jnp.where(here_too, 0, jnp.where(source == me ^ 1, 1, 2))
        codes[i] = jnp.full(codes.shape[1:], code, jnp.int32)
        put(rest, 1 + i, twice(coupling[kind]))


def near_kernel(live, targets, sources, window, after, tiles, blocks, gathered, places, near, links, right):
    for i in range(links.shape[0]):
        links[i] = gathered[jnp.max(places[i])]
    slots, points, _ = tiles.shape
    boxes = near.shape[0]
    for b in range(boxes):
        right[b] = after[:, b * points : (b + 1) * points]
    near[...] = jnp.zeros_like(near)
    for slot in range(slots):
        box = sources[slot]
        inner = window[jnp.minimum(box, 2 * boxes - 1)]
        outer = right[jnp.maximum(box - 2 * boxes, 0)]
        source = jnp.where(box < 2 * boxes, inner, outer)
        source = jnp.where(slot < live[0], source, jnp.zeros_like(source))
        target = targets[slot]
        near[target] = near[target] + dot(source, tiles[slot])


def half_kernel(bits, device, gathered, maps, send, total):
    count = gathered.shape[0]
    wide = 2 * maps.shape[1]
    me = device[0]

    def step(k):
        coeffs = jnp.concatenate([gathered[2 * k], gathered[2 * k + 1]], axis=1)
        return dot(coeffs, maps[pl.ds(k * wide, wide)])

    pairs = count // 2
    if pairs <= 32:
        both = step(0)
        for k in range(1, pairs):
            both = both + step(k)
    else:
        both = lax.fori_loop(1, pairs, lambda k, sums: sums + step(k), step(0))
    sums = both_halves(both)
    total[...] = sums
    across = (me + jnp.where((me & 1) == 1, -2, 2)) & (2**bits - 1)
    send[0] = gathered[0]
    send[1] = gathered[place_of(across >> 1, me >> 1, bits - 1)]
    send[2] = high_low(sums)


def field_kernel(other, links, codes, rest, total, spread, local, basis, near, field):
    boxes, rank, points = basis.shape
    parts = [other[0]]
    for i in range(links.shape[0]):
        code = codes[i]
        elsewhere = jnp.where(code == 1, other[0].astype(F32), other[1].astype(F32))
        parts.append(jnp.where(code == 0, links[i].astype(F32), elsewhere).astype(BF16))
    mine = both_halves(dot(jnp.concatenate(parts, axis=1), rest[...]))
    pair = total[...] + both_halves(other[2].astype(F32))
    doubled = dot(jnp.concatenate([high_low(pair), high_low(mine)], axis=1), spread[...], NT)
    half = boxes * rank
    rounded = (doubled[:, :half] + doubled[:, half:] + local[...]).astype(BF16)
    for b in range(boxes):
        far = dot(rounded[:, b * rank : (b + 1) * rank], basis[b])
        field[:, b * points : (b + 1) * points] = near[b] + far


SPACES = {"v": pltpu.VMEM, "s": pltpu.SMEM, "h": pl.ANY}


def call(kernel, name, kinds, args, outs, scratch=(), flops=0):
    moved = sum(x.size * x.dtype.itemsize for x in args)
    held = [x for x, kind in zip(args, kinds) if kind == "v"]
    held += [jax.ShapeDtypeStruct(shape, kind) for space, shape, kind in outs if space == "v"]
    limit = STACK + sum(x.size // x.shape[-1] * max(x.shape[-1], 128) * x.dtype.itemsize for x in held)
    args = [
        pltpu.with_memory_space_constraint(x, pltpu.HBM) if kind == "h" else x
        for kind, x in zip(kinds, args)
    ]
    return pl.pallas_call(
        kernel,
        name=name,
        out_shape=[jax.ShapeDtypeStruct(shape, kind) for _, shape, kind in outs],
        in_specs=[pl.BlockSpec(memory_space=SPACES[kind]) for kind in kinds],
        out_specs=[pl.BlockSpec(memory_space=SPACES[space]) for space, _, _ in outs],
        scratch_shapes=list(scratch),
        compiler_params=pltpu.CompilerParams(vmem_limit_bytes=limit),
        cost_estimate=pl.CostEstimate(flops=flops, bytes_accessed=moved, transcendentals=0),
    )(*args)


def body(
    vectors,
    leaf_basis,
    transfer,
    sibling_coupling,
    list_coupling,
    near_tiles,
    tile_target,
    tile_source,
    tile_count,
    couple_offset,
    couple_class,
):
    columns, width = vectors.shape
    boxes, rank, points = leaf_basis.shape
    count = lax.axis_size(AXES)
    bits = count.bit_length() - 1
    steps = boxes.bit_length() - 1
    double = 2 * rank
    dma = pltpu.SemaphoreType.DMA

    def send(x, target):
        return lax.ppermute(x, AXES, [(i, target(i)) for i in range(count)])

    def turned(i, low, wide, step):
        digit = (i >> low) % 2**wide
        return i + (((digit + step) % 2**wide - digit) << low)

    before = send(vectors, lambda i: (i + 1) % count)
    ints = jnp.int32
    plain = (transfer, vectors, sibling_coupling)
    path_shapes = [(2 ** (height - 1), 2, rank, double) for height in range(1, steps + 1)]
    transfer, own, sibling, coeffs, leaf, *paths = call(
        leaf_kernel,
        "leaf",
        "hhhh",
        (*plain, leaf_basis),
        (
            *(("v", x.shape, x.dtype) for x in plain),
            ("v", (1, columns, double), BF16),
            ("v", (boxes, columns, rank), F32),
            *(("v", shape, F32) for shape in path_shapes),
        ),
        scratch=(pltpu.VMEM(leaf_basis.shape, BF16), dma((4,))),
    )
    device = lax.axis_index(AXES).astype(ints).reshape(1)
    window, passed = call(
        window_kernel,
        "window",
        "vvv",
        (coeffs, before, own),
        (("v", (2 * boxes, columns, points), BF16), ("v", coeffs.shape, BF16)),
    )
    lists = (tile_target, tile_source, couple_offset, couple_class)
    links = couple_offset.shape[1]
    gathered = coeffs
    after = send(own, lambda i: (i - 1) % count)
    for index, (low, wide) in enumerate(rounds_of(bits - 1)):
        kept = passed if index == 0 else gathered
        if index == 1:
            maps, rest, places, codes, kept, spread, local, targets, sources = call(
                functools.partial(map_kernel, bits),
                "maps",
                "shhhhhvvvv" + "v" * steps,
                (device, *lists, list_coupling, gathered, transfer, sibling, leaf, *paths),
                (
                    ("v", (count // 2 * double, double), BF16),
                    ("v", ((1 + links) * double, double), BF16),
                    ("v", (links, 8, 128), ints),
                    ("v", (links, columns, double), ints),
                    ("v", gathered.shape, BF16),
                    ("v", (2 * boxes * rank, 2 * double), BF16),
                    ("v", (columns, boxes * rank), F32),
                    ("v", tile_target.shape, ints),
                    ("v", tile_source.shape, ints),
                ),
                scratch=(
                    pltpu.SMEM(couple_offset.shape, ints),
                    pltpu.SMEM(couple_class.shape, ints),
                    pltpu.VMEM(list_coupling.shape, F32),
                    dma((5,)),
                ),
            )
        parts = [kept]
        for step in range(1, 2**wide):
            parts.append(send(gathered, lambda i, args=(low + 1, wide, step): turned(i, *args)))
        gathered = jnp.concatenate(parts, axis=0)
    blocks, total = call(
        functools.partial(half_kernel, bits),
        "half",
        "svv",
        (device, gathered, maps),
        (("v", (3, columns, double), BF16), ("v", (columns, double), F32)),
    )
    other = send(blocks, lambda i: i ^ 1)
    near, picked = call(
        near_kernel,
        "near",
        "sssvvvvvv",
        (tile_count, targets, sources, window, after, near_tiles, blocks, gathered, places),
        (("v", (boxes, columns, points), F32), ("v", (links, columns, double), BF16)),
        scratch=(pltpu.VMEM((boxes, columns, points), BF16),),
    )
    (field,) = call(
        field_kernel,
        "field",
        "v" * 9,
        (other, picked, codes, rest, total, spread, local, leaf_basis, near),
        (("v", (columns, width), F32),),
    )
    return field


def solution(mesh):
    in_specs = (
        P(None, AXES),
        P(AXES, None, None),
        P(),
        P(),
        P(),
        P(AXES, None, None),
        P(AXES),
        P(AXES),
        P(AXES),
        P(AXES, None),
        P(AXES, None),
    )
    return jax.shard_map(body, mesh=mesh, in_specs=in_specs, out_specs=P(None, AXES), check_vma=False)
```

```python
import functools

import jax
import jax.numpy as jnp
from jax import lax
from jax.experimental import pallas as pl
from jax.experimental.pallas import tpu as pltpu
from jax.sharding import PartitionSpec as P

AXES = ("leaf", "grp")
F32 = jnp.float32
BF16 = jnp.bfloat16
NN = (((1,), (0,)), ((), ()))
NT = (((1,), (1,)), ((), ()))
CHUNK = 512
STACK = 6 * 2**20


def split(x):
    high = x.astype(BF16)
    return high, (x - high.astype(F32)).astype(BF16)


def dot(a, b, dims=NN):
    return lax.dot_general(a, b, dims, preferred_element_type=F32)


def dot3(a, b, dims=NN):
    a_high, a_low = split(a)
    b_high, b_low = split(b)
    return dot(a_high, b_high, dims) + (dot(a_low, b_high, dims) + dot(a_high, b_low, dims))


def rounds_of(bits):
    rounds = []
    top = bits
    while top > 0:
        wide = 2 if top > 1 else 1
        rounds.append((top - wide, wide))
        top -= wide
    return rounds


def place_of(source, here, bits):
    place, shift = 0, 0
    for low, wide in rounds_of(bits):
        place = place | ((((here >> low) - (source >> low)) & (2**wide - 1)) << shift)
        shift += wide
    return place


def up(blocks, transfer):
    left = jnp.concatenate(blocks[0::2], axis=0)
    right = jnp.concatenate(blocks[1::2], axis=0)
    rows = blocks[0].shape[0]
    total = dot3(left, transfer[0]) + dot3(right, transfer[1])
    return [total[i * rows : (i + 1) * rows] for i in range(len(blocks) // 2)]


def high_low(double):
    high, low = split(double)
    lane = lax.broadcasted_iota(jnp.int32, double.shape, 1)
    return jnp.where(lane < double.shape[1] // 2, high, low)


def twice(x):
    return jnp.concatenate([x, x], axis=1)


def both_halves(x):
    return x + pltpu.roll(x, x.shape[1] // 2, 1)


def packed(double):
    high, low = split(double)
    lane = lax.broadcasted_iota(jnp.int32, double.shape, 1)
    return jnp.concatenate([jnp.where(lane < double.shape[1] // 2, high, low), high], axis=1)


def packing(right):
    high, low = split(right)
    return jnp.concatenate([high, high, low, jnp.zeros_like(low)], axis=0)


def start_copies(pairs, sems):
    copies = [pltpu.make_async_copy(a, b, sems.at[i]) for i, (a, b) in enumerate(pairs)]
    for copy in copies:
        copy.start()
    return copies


def leaf_kernel(transfer_hbm, vectors_hbm, sibling_hbm, basis_hbm, transfer, vectors, sibling, send, leaf, *refs):
    *paths, basis, sems = refs
    boxes, rank, points = basis.shape
    steps = boxes.bit_length() - 1
    pairs = ((transfer_hbm, transfer), (vectors_hbm, vectors), (basis_hbm, basis), (sibling_hbm, sibling))
    copies = start_copies(pairs, sems)
    copies[0].wait()
    t0, t1 = twice(transfer[0]), twice(transfer[1])
    double = jnp.concatenate([t0, t1], axis=0)
    sides = packing(jnp.concatenate([t0, t1], axis=1))
    for height in range(1, steps + 1):
        if height == steps:
            copies[1].wait()
            copies[2].wait()
            high, low = [], []
            for b in range(boxes):
                coeffs = dot(vectors[:, b * points : (b + 1) * points], basis[b], NT)
                leaf[b] = coeffs
                one, other = split(coeffs)
                high.append(one)
                low.append(other)
        if height > 1:
            wide = dot(packed(double), sides)
            double = jnp.concatenate([wide[:, : 2 * rank], wide[:, 2 * rank :]], axis=0)
        paths[height - 1][...] = double.reshape(paths[height - 1].shape)
    weights = jnp.concatenate(split(double), axis=1)
    high = jnp.concatenate(high, axis=1)
    low = jnp.concatenate(low, axis=1)
    sums = dot(high, weights)
    sums = sums[:, : 2 * rank] + (sums[:, 2 * rank :] + dot(low, weights[:, : 2 * rank]))
    send[0] = high_low(sums)
    copies[3].wait()


def window_kernel(coeffs, before, own, window, passed):
    passed[...] = coeffs[...]
    boxes = window.shape[0] // 2
    points = window.shape[2]
    for i, part in enumerate((before, own)):
        for b in range(boxes):
            window[i * boxes + b] = part[:, b * points : (b + 1) * points]


def fill_down(me, leaf, paths, transfer, sibling, spread, local):
    boxes, columns, rank = leaf.shape
    half = boxes * rank
    t0, t1 = transfer[0], transfer[1]
    s0, s1 = sibling[0], sibling[1]
    tall = paths[...].reshape(half, 2 * rank)
    high, low = split(tall)
    spread[:half, 2 * rank :] = high
    spread[half:, 2 * rank :] = low
    high, low = split(dot(packed(tall), packing(twice(transfer[me & 1]))))
    spread[:half, : 2 * rank] = high
    spread[half:, : 2 * rank] = low
    levels = [[leaf[b] for b in range(boxes)]]
    while len(levels[-1]) > 2:
        levels.append(up(levels[-1], (t0, t1)))
    down = None
    for level in reversed(levels):
        across0 = dot3(jnp.concatenate(level[1::2], axis=0), s0)
        across1 = dot3(jnp.concatenate(level[0::2], axis=0), s1)
        if down is not None:
            parents = jnp.concatenate(down, axis=0)
            across0 = across0 + dot3(parents, t0, NT)
            across1 = across1 + dot3(parents, t1, NT)
        down = []
        for i in range(len(level) // 2):
            down.append(across0[i * columns : (i + 1) * columns])
            down.append(across1[i * columns : (i + 1) * columns])
    for b in range(boxes):
        local[:, b * rank : (b + 1) * rank] = down[b]


def map_kernel(bits, device, *refs):
    hbm, (gathered, transfer, sibling, leaf), paths = refs[:5], refs[5:9], refs[9:-13]
    maps, rest, places, codes, passed, spread, local, *here, sems = refs[-13:]
    copies = start_copies(zip(hbm, here), sems)
    _, _, offsets, classes, coupling = here
    rank = transfer.shape[1]
    passed[...] = gathered[...]
    me = device[0]
    side = me & 1
    pair = me >> 1
    count = 2**bits
    steps = len(paths)

    def put(table, at, double):
        both = high_low(double)
        if isinstance(at, int):
            at = at * 2 * rank
        else:
            at = pl.multiple_of(at * 2 * rank, 2 * rank)
        table[pl.ds(at, rank)] = both
        table[pl.ds(at + rank, rank)] = both

    def place(height, low):
        return place_of((((pair >> height) ^ 1) << height) | low, pair, bits - 1)

    sides = []
    for height in range(1, steps + 1):
        tall = paths[height - 1][:, side].reshape(2 ** (height - 1) * rank, 2 * rank)
        sides.append(packed(tall))

    def climb(height, fan):
        return dot(sides[height - 1], packing(fan))

    t0, t1 = transfer[0], transfer[1]

    def path(height):
        if height <= steps:
            low = pair & ((1 << height) - 1)
            return paths[height - 1][low >> 1, low & 1][:, :rank]
        return dot3(path(height - 1), transfer[(pair >> (height - 1)) & 1])

    put(maps, 0, jnp.zeros((rank, 2 * rank), F32))
    wide = []
    for height in range(1, bits):
        bridge = sibling[(me >> height) & 1]
        if height > 1:
            bridge = dot3(bridge, path(height - 1), NT)
        fans = [twice(bridge)]
        for _ in range(height - steps):
            fans = [dot3(t, fan) for fan in fans for t in (t0, t1)]
        if height < steps:
            block = climb(height, fans[0])
            for i in range(2 ** (height - 1)):
                put(maps, place(height - 1, i), block[i * rank : (i + 1) * rank])
        else:
            wide += [(height, j, fan) for j, fan in enumerate(fans)]
    for start in range(0, len(wide), 4):
        part = wide[start : start + 4]
        block = climb(steps, jnp.concatenate([fan for _, _, fan in part], axis=1))
        for k, (height, j, _) in enumerate(part):
            for i in range(2 ** (steps - 1)):
                one = block[i * rank : (i + 1) * rank, k * 2 * rank : (k + 1) * 2 * rank]
                put(maps, place(height - 1, (j << (steps - 1)) + i), one)
    put(rest, 0, twice(sibling[side]))
    fill_down(me, leaf, paths[-1], transfer, sibling, spread, local)
    for copy in copies:
        copy.wait()
    for i in range(offsets.shape[1]):
        offset = offsets[0, i]
        kind = classes[0, i]
        source = (me + offset + count) & (count - 1)
        here_too = ((source ^ me) & 1) == 0
        link = jnp.where(here_too, place_of(source >> 1, pair, bits - 1), 0)
        places[i] = jnp.full(places.shape[1:], link, jnp.int32)
        code = jnp.where(here_too, 0, jnp.where(source == me ^ 1, 1, 2))
        codes[i] = jnp.full(codes.shape[1:], code, jnp.int32)
        put(rest, 1 + i, twice(coupling[kind]))


def near_kernel(live, targets, sources, window, after, tiles, blocks, gathered, places, near, links, right):
    for i in range(links.shape[0]):
        links[i] = gathered[jnp.max(places[i])]
    slots, points, _ = tiles.shape
    boxes = near.shape[0]
    for b in range(boxes):
        right[b] = after[:, b * points : (b + 1) * points]
    near[...] = jnp.zeros_like(near)
    for slot in range(slots):
        box = sources[slot]
        inner = window[jnp.minimum(box, 2 * boxes - 1)]
        outer = right[jnp.maximum(box - 2 * boxes, 0)]
        source = jnp.where(box < 2 * boxes, inner, outer)
        source = jnp.where(slot < live[0], source, jnp.zeros_like(source))
        target = targets[slot]
        near[target] = near[target] + dot(source, tiles[slot])


def half_kernel(bits, device, gathered, maps, send, total):
    count = gathered.shape[0]
    wide = 2 * maps.shape[1]
    me = device[0]

    def step(k):
        coeffs = jnp.concatenate([gathered[2 * k], gathered[2 * k + 1]], axis=1)
        return dot(coeffs, maps[pl.ds(k * wide, wide)])

    pairs = count // 2
    if pairs <= 32:
        both = step(0)
        for k in range(1, pairs):
            both = both + step(k)
    else:
        both = lax.fori_loop(1, pairs, lambda k, sums: sums + step(k), step(0))
    sums = both_halves(both)
    total[...] = sums
    across = (me + jnp.where((me & 1) == 1, -2, 2)) & (2**bits - 1)
    send[0] = gathered[0]
    send[1] = gathered[place_of(across >> 1, me >> 1, bits - 1)]
    send[2] = high_low(sums)


def field_kernel(other, links, codes, rest, total, spread, local, basis, near, field):
    boxes, rank, points = basis.shape
    parts = [other[0]]
    for i in range(links.shape[0]):
        code = codes[i]
        elsewhere = jnp.where(code == 1, other[0].astype(F32), other[1].astype(F32))
        parts.append(jnp.where(code == 0, links[i].astype(F32), elsewhere).astype(BF16))
    mine = both_halves(dot(jnp.concatenate(parts, axis=1), rest[...]))
    pair = total[...] + both_halves(other[2].astype(F32))
    doubled = dot(jnp.concatenate([high_low(pair), high_low(mine)], axis=1), spread[...], NT)
    half = boxes * rank
    rounded = (doubled[:, :half] + doubled[:, half:] + local[...]).astype(BF16)
    columns = near.shape[1]
    lane = lax.broadcasted_iota(jnp.int32, (columns, 2 * rank), 1)
    for b in range(0, boxes, 2):
        both = rounded[:, b * rank : (b + 2) * rank]
        zeros = jnp.zeros_like(both)
        apart = [jnp.where(lane < rank, both, zeros), jnp.where(lane < rank, zeros, both)]
        far = dot(jnp.concatenate(apart, axis=0), basis[b : b + 2].reshape(2 * rank, points))
        field[:, b * points : (b + 1) * points] = near[b] + far[:columns]
        field[:, (b + 1) * points : (b + 2) * points] = near[b + 1] + far[columns:]


SPACES = {"v": pltpu.VMEM, "s": pltpu.SMEM, "h": pl.ANY}


def call(kernel, name, kinds, args, outs, scratch=(), flops=0):
    moved = sum(x.size * x.dtype.itemsize for x in args)
    held = [x for x, kind in zip(args, kinds) if kind == "v"]
    held += [jax.ShapeDtypeStruct(shape, kind) for space, shape, kind in outs if space == "v"]
    limit = STACK + sum(x.size // x.shape[-1] * max(x.shape[-1], 128) * x.dtype.itemsize for x in held)
    args = [
        pltpu.with_memory_space_constraint(x, pltpu.HBM) if kind == "h" else x
        for kind, x in zip(kinds, args)
    ]
    return pl.pallas_call(
        kernel,
        name=name,
        out_shape=[jax.ShapeDtypeStruct(shape, kind) for _, shape, kind in outs],
        in_specs=[pl.BlockSpec(memory_space=SPACES[kind]) for kind in kinds],
        out_specs=[pl.BlockSpec(memory_space=SPACES[space]) for space, _, _ in outs],
        scratch_shapes=list(scratch),
        compiler_params=pltpu.CompilerParams(vmem_limit_bytes=limit),
        cost_estimate=pl.CostEstimate(flops=flops, bytes_accessed=moved, transcendentals=0),
    )(*args)


def body(
    vectors,
    leaf_basis,
    transfer,
    sibling_coupling,
    list_coupling,
    near_tiles,
    tile_target,
    tile_source,
    tile_count,
    couple_offset,
    couple_class,
):
    columns, width = vectors.shape
    boxes, rank, points = leaf_basis.shape
    count = lax.axis_size(AXES)
    bits = count.bit_length() - 1
    steps = boxes.bit_length() - 1
    double = 2 * rank
    dma = pltpu.SemaphoreType.DMA

    def send(x, target):
        return lax.ppermute(x, AXES, [(i, target(i)) for i in range(count)])

    def turned(i, low, wide, step):
        digit = (i >> low) % 2**wide
        return i + (((digit + step) % 2**wide - digit) << low)

    before = send(vectors, lambda i: (i + 1) % count)
    ints = jnp.int32
    plain = (transfer, vectors, sibling_coupling)
    path_shapes = [(2 ** (height - 1), 2, rank, double) for height in range(1, steps + 1)]
    transfer, own, sibling, coeffs, leaf, *paths = call(
        leaf_kernel,
        "leaf",
        "hhhh",
        (*plain, leaf_basis),
        (
            *(("v", x.shape, x.dtype) for x in plain),
            ("v", (1, columns, double), BF16),
            ("v", (boxes, columns, rank), F32),
            *(("v", shape, F32) for shape in path_shapes),
        ),
        scratch=(pltpu.VMEM(leaf_basis.shape, BF16), dma((4,))),
    )
    device = lax.axis_index(AXES).astype(ints).reshape(1)
    window, passed = call(
        window_kernel,
        "window",
        "vvv",
        (coeffs, before, own),
        (("v", (2 * boxes, columns, points), BF16), ("v", coeffs.shape, BF16)),
    )
    lists = (tile_target, tile_source, couple_offset, couple_class)
    links = couple_offset.shape[1]
    gathered = coeffs
    after = send(own, lambda i: (i - 1) % count)
    for index, (low, wide) in enumerate(rounds_of(bits - 1)):
        kept = passed if index == 0 else gathered
        if index == 1:
            maps, rest, places, codes, kept, spread, local, targets, sources = call(
                functools.partial(map_kernel, bits),
                "maps",
                "shhhhhvvvv" + "v" * steps,
                (device, *lists, list_coupling, gathered, transfer, sibling, leaf, *paths),
                (
                    ("v", (count // 2 * double, double), BF16),
                    ("v", ((1 + links) * double, double), BF16),
                    ("v", (links, 8, 128), ints),
                    ("v", (links, columns, double), ints),
                    ("v", gathered.shape, BF16),
                    ("v", (2 * boxes * rank, 2 * double), BF16),
                    ("v", (columns, boxes * rank), F32),
                    ("v", tile_target.shape, ints),
                    ("v", tile_source.shape, ints),
                ),
                scratch=(
                    pltpu.SMEM(couple_offset.shape, ints),
                    pltpu.SMEM(couple_class.shape, ints),
                    pltpu.VMEM(list_coupling.shape, F32),
                    dma((5,)),
                ),
            )
        parts = [kept]
        for step in range(1, 2**wide):
            parts.append(send(gathered, lambda i, args=(low + 1, wide, step): turned(i, *args)))
        gathered = jnp.concatenate(parts, axis=0)
    blocks, total = call(
        functools.partial(half_kernel, bits),
        "half",
        "svv",
        (device, gathered, maps),
        (("v", (3, columns, double), BF16), ("v", (columns, double), F32)),
    )
    other = send(blocks, lambda i: i ^ 1)
    near, picked = call(
        near_kernel,
        "near",
        "sssvvvvvv",
        (tile_count, targets, sources, window, after, near_tiles, blocks, gathered, places),
        (("v", (boxes, columns, points), F32), ("v", (links, columns, double), BF16)),
        scratch=(pltpu.VMEM((boxes, columns, points), BF16),),
    )
    (field,) = call(
        field_kernel,
        "field",
        "v" * 9,
        (other, picked, codes, rest, total, spread, local, leaf_basis, near),
        (("v", (columns, width), F32),),
    )
    return field


def solution(mesh):
    in_specs = (
        P(None, AXES),
        P(AXES, None, None),
        P(),
        P(),
        P(),
        P(AXES, None, None),
        P(AXES),
        P(AXES),
        P(AXES),
        P(AXES, None),
        P(AXES, None),
    )
    return jax.shard_map(body, mesh=mesh, in_specs=in_specs, out_specs=P(None, AXES), check_vma=False)
```

```python
import functools

import jax
import jax.numpy as jnp
from jax import lax
from jax.experimental import pallas as pl
from jax.experimental.pallas import tpu as pltpu
from jax.sharding import PartitionSpec as P

AXES = ("leaf", "grp")
F32 = jnp.float32
BF16 = jnp.bfloat16
NN = (((1,), (0,)), ((), ()))
NT = (((1,), (1,)), ((), ()))
CHUNK = 512
STACK = 6 * 2**20


def split(x):
    high = x.astype(BF16)
    return high, (x - high.astype(F32)).astype(BF16)


def dot(a, b, dims=NN):
    return lax.dot_general(a, b, dims, preferred_element_type=F32)


def dot3(a, b, dims=NN):
    a_high, a_low = split(a)
    b_high, b_low = split(b)
    return dot(a_high, b_high, dims) + (dot(a_low, b_high, dims) + dot(a_high, b_low, dims))


def rounds_of(bits):
    rounds = []
    top = bits
    while top > 0:
        wide = 2 if top > 1 else 1
        rounds.append((top - wide, wide))
        top -= wide
    return rounds


def place_of(source, here, bits):
    place, shift = 0, 0
    for low, wide in rounds_of(bits):
        place = place | ((((here >> low) - (source >> low)) & (2**wide - 1)) << shift)
        shift += wide
    return place


def up(blocks, transfer):
    left = jnp.concatenate(blocks[0::2], axis=0)
    right = jnp.concatenate(blocks[1::2], axis=0)
    rows = blocks[0].shape[0]
    total = dot3(left, transfer[0]) + dot3(right, transfer[1])
    return [total[i * rows : (i + 1) * rows] for i in range(len(blocks) // 2)]


def high_low(double):
    high, low = split(double)
    lane = lax.broadcasted_iota(jnp.int32, double.shape, 1)
    return jnp.where(lane < double.shape[1] // 2, high, low)


def twice(x):
    return jnp.concatenate([x, x], axis=1)


def both_halves(x):
    return x + pltpu.roll(x, x.shape[1] // 2, 1)


def packed(double):
    high, low = split(double)
    lane = lax.broadcasted_iota(jnp.int32, double.shape, 1)
    return jnp.concatenate([jnp.where(lane < double.shape[1] // 2, high, low), high], axis=1)


def packing(right):
    high, low = split(right)
    return jnp.concatenate([high, high, low, jnp.zeros_like(low)], axis=0)


def start_copies(pairs, sems):
    copies = [pltpu.make_async_copy(a, b, sems.at[i]) for i, (a, b) in enumerate(pairs)]
    for copy in copies:
        copy.start()
    return copies


def leaf_kernel(transfer_hbm, vectors_hbm, sibling_hbm, basis_hbm, transfer, vectors, sibling, send, leaf, *refs):
    *paths, basis, sems = refs
    boxes, rank, points = basis.shape
    steps = boxes.bit_length() - 1
    first, second = pl.ds(0, boxes // 2), pl.ds(boxes // 2, boxes // 2)
    pairs = [(transfer_hbm, transfer), (vectors_hbm, vectors), (basis_hbm.at[first], basis.at[first])]
    pairs += [(sibling_hbm, sibling), (basis_hbm.at[second], basis.at[second])]
    copies = start_copies(pairs, sems)
    copies[0].wait()
    t0, t1 = twice(transfer[0]), twice(transfer[1])
    double = jnp.concatenate([t0, t1], axis=0)
    sides = packing(jnp.concatenate([t0, t1], axis=1))
    for height in range(1, steps + 1):
        if height == steps:
            copies[1].wait()
            copies[2].wait()
            copies[4].wait()
            high, low = [], []
            for b in range(boxes):
                coeffs = dot(vectors[:, b * points : (b + 1) * points], basis[b], NT)
                leaf[b] = coeffs
                one, other = split(coeffs)
                high.append(one)
                low.append(other)
        if height > 1:
            wide = dot(packed(double), sides)
            double = jnp.concatenate([wide[:, : 2 * rank], wide[:, 2 * rank :]], axis=0)
        paths[height - 1][...] = double.reshape(paths[height - 1].shape)
    weights = jnp.concatenate(split(double), axis=1)
    high = jnp.concatenate(high, axis=1)
    low = jnp.concatenate(low, axis=1)
    sums = dot(high, weights)
    sums = sums[:, : 2 * rank] + (sums[:, 2 * rank :] + dot(low, weights[:, : 2 * rank]))
    send[0] = high_low(sums)
    copies[3].wait()


def window_kernel(coeffs, before, own, window, passed):
    passed[...] = coeffs[...]
    boxes = window.shape[0] // 2
    points = window.shape[2]
    for i, part in enumerate((before, own)):
        for b in range(boxes):
            window[i * boxes + b] = part[:, b * points : (b + 1) * points]


def fill_down(me, leaf, paths, transfer, sibling, spread, local):
    boxes, columns, rank = leaf.shape
    half = boxes * rank
    t0, t1 = transfer[0], transfer[1]
    s0, s1 = sibling[0], sibling[1]
    tall = paths[...].reshape(half, 2 * rank)
    high, low = split(tall)
    spread[:half, 2 * rank :] = high
    spread[half:, 2 * rank :] = low
    high, low = split(dot(packed(tall), packing(twice(transfer[me & 1]))))
    spread[:half, : 2 * rank] = high
    spread[half:, : 2 * rank] = low
    levels = [[leaf[b] for b in range(boxes)]]
    while len(levels[-1]) > 2:
        levels.append(up(levels[-1], (t0, t1)))
    down = None
    for level in reversed(levels):
        across0 = dot3(jnp.concatenate(level[1::2], axis=0), s0)
        across1 = dot3(jnp.concatenate(level[0::2], axis=0), s1)
        if down is not None:
            parents = jnp.concatenate(down, axis=0)
            across0 = across0 + dot3(parents, t0, NT)
            across1 = across1 + dot3(parents, t1, NT)
        down = []
        for i in range(len(level) // 2):
            down.append(across0[i * columns : (i + 1) * columns])
            down.append(across1[i * columns : (i + 1) * columns])
    for b in range(boxes):
        local[:, b * rank : (b + 1) * rank] = down[b]


def map_kernel(bits, device, *refs):
    hbm, (gathered, transfer, sibling, leaf), paths = refs[:5], refs[5:9], refs[9:-13]
    maps, rest, places, codes, passed, spread, local, *here, sems = refs[-13:]
    copies = start_copies(zip(hbm, here), sems)
    _, _, offsets, classes, coupling = here
    rank = transfer.shape[1]
    passed[...] = gathered[...]
    me = device[0]
    side = me & 1
    pair = me >> 1
    count = 2**bits
    steps = len(paths)

    def put(table, at, double):
        both = high_low(double)
        if isinstance(at, int):
            at = at * 2 * rank
        else:
            at = pl.multiple_of(at * 2 * rank, 2 * rank)
        table[pl.ds(at, rank)] = both
        table[pl.ds(at + rank, rank)] = both

    def place(height, low):
        return place_of((((pair >> height) ^ 1) << height) | low, pair, bits - 1)

    sides = []
    for height in range(1, steps + 1):
        tall = paths[height - 1][:, side].reshape(2 ** (height - 1) * rank, 2 * rank)
        sides.append(packed(tall))

    def climb(height, fan):
        return dot(sides[height - 1], packing(fan))

    t0, t1 = transfer[0], transfer[1]

    def path(height):
        if height <= steps:
            low = pair & ((1 << height) - 1)
            return paths[height - 1][low >> 1, low & 1][:, :rank]
        return dot3(path(height - 1), transfer[(pair >> (height - 1)) & 1])

    put(maps, 0, jnp.zeros((rank, 2 * rank), F32))
    wide = []
    for height in range(1, bits):
        bridge = sibling[(me >> height) & 1]
        if height > 1:
            bridge = dot3(bridge, path(height - 1), NT)
        fans = [twice(bridge)]
        for _ in range(height - steps):
            fans = [dot3(t, fan) for fan in fans for t in (t0, t1)]
        if height < steps:
            block = climb(height, fans[0])
            for i in range(2 ** (height - 1)):
                put(maps, place(height - 1, i), block[i * rank : (i + 1) * rank])
        else:
            wide += [(height, j, fan) for j, fan in enumerate(fans)]
    for start in range(0, len(wide), 4):
        part = wide[start : start + 4]
        block = climb(steps, jnp.concatenate([fan for _, _, fan in part], axis=1))
        for k, (height, j, _) in enumerate(part):
            for i in range(2 ** (steps - 1)):
                one = block[i * rank : (i + 1) * rank, k * 2 * rank : (k + 1) * 2 * rank]
                put(maps, place(height - 1, (j << (steps - 1)) + i), one)
    put(rest, 0, twice(sibling[side]))
    fill_down(me, leaf, paths[-1], transfer, sibling, spread, local)
    for copy in copies:
        copy.wait()
    for i in range(offsets.shape[1]):
        offset = offsets[0, i]
        kind = classes[0, i]
        source = (me + offset + count) & (count - 1)
        here_too = ((source ^ me) & 1) == 0
        link = jnp.where(here_too, place_of(source >> 1, pair, bits - 1), 0)
        places[i] = jnp.full(places.shape[1:], link, jnp.int32)
        code = jnp.where(here_too, 0, jnp.where(source == me ^ 1, 1, 2))
        codes[i] = jnp.full(codes.shape[1:], code, jnp.int32)
        put(rest, 1 + i, twice(coupling[kind]))


def near_kernel(live, targets, sources, window, after, tiles, blocks, gathered, places, near, links, right):
    for i in range(links.shape[0]):
        links[i] = gathered[jnp.max(places[i])]
    slots, points, _ = tiles.shape
    boxes = near.shape[0]
    for b in range(boxes):
        right[b] = after[:, b * points : (b + 1) * points]
    near[...] = jnp.zeros_like(near)
    for slot in range(slots):
        box = sources[slot]
        inner = window[jnp.minimum(box, 2 * boxes - 1)]
        outer = right[jnp.maximum(box - 2 * boxes, 0)]
        source = jnp.where(box < 2 * boxes, inner, outer)
        source = jnp.where(slot < live[0], source, jnp.zeros_like(source))
        target = targets[slot]
        near[target] = near[target] + dot(source, tiles[slot])


def half_kernel(bits, device, gathered, maps, send, total):
    count = gathered.shape[0]
    wide = 2 * maps.shape[1]
    me = device[0]

    def step(k):
        coeffs = jnp.concatenate([gathered[2 * k], gathered[2 * k + 1]], axis=1)
        return dot(coeffs, maps[pl.ds(k * wide, wide)])

    pairs = count // 2
    if pairs <= 32:
        both = step(0)
        for k in range(1, pairs):
            both = both + step(k)
    else:
        both = lax.fori_loop(1, pairs, lambda k, sums: sums + step(k), step(0))
    sums = both_halves(both)
    total[...] = sums
    across = (me + jnp.where((me & 1) == 1, -2, 2)) & (2**bits - 1)
    send[0] = gathered[0]
    send[1] = gathered[place_of(across >> 1, me >> 1, bits - 1)]
    send[2] = high_low(sums)


def field_kernel(other, links, codes, rest, total, spread, local, basis, near, field):
    boxes, rank, points = basis.shape
    parts = [other[0]]
    for i in range(links.shape[0]):
        code = codes[i]
        elsewhere = jnp.where(code == 1, other[0].astype(F32), other[1].astype(F32))
        parts.append(jnp.where(code == 0, links[i].astype(F32), elsewhere).astype(BF16))
    mine = both_halves(dot(jnp.concatenate(parts, axis=1), rest[...]))
    pair = total[...] + both_halves(other[2].astype(F32))
    doubled = dot(jnp.concatenate([high_low(pair), high_low(mine)], axis=1), spread[...], NT)
    half = boxes * rank
    rounded = (doubled[:, :half] + doubled[:, half:] + local[...]).astype(BF16)
    columns = near.shape[1]
    lane = lax.broadcasted_iota(jnp.int32, (columns, 2 * rank), 1)
    for b in range(0, boxes, 2):
        both = rounded[:, b * rank : (b + 2) * rank]
        zeros = jnp.zeros_like(both)
        apart = [jnp.where(lane < rank, both, zeros), jnp.where(lane < rank, zeros, both)]
        far = dot(jnp.concatenate(apart, axis=0), basis[b : b + 2].reshape(2 * rank, points))
        field[:, b * points : (b + 1) * points] = near[b] + far[:columns]
        field[:, (b + 1) * points : (b + 2) * points] = near[b + 1] + far[columns:]


SPACES = {"v": pltpu.VMEM, "s": pltpu.SMEM, "h": pl.ANY}


def call(kernel, name, kinds, args, outs, scratch=(), flops=0):
    moved = sum(x.size * x.dtype.itemsize for x in args)
    held = [x for x, kind in zip(args, kinds) if kind == "v"]
    held += [jax.ShapeDtypeStruct(shape, kind) for space, shape, kind in outs if space == "v"]
    limit = STACK + sum(x.size // x.shape[-1] * max(x.shape[-1], 128) * x.dtype.itemsize for x in held)
    args = [
        pltpu.with_memory_space_constraint(x, pltpu.HBM) if kind == "h" else x
        for kind, x in zip(kinds, args)
    ]
    return pl.pallas_call(
        kernel,
        name=name,
        out_shape=[jax.ShapeDtypeStruct(shape, kind) for _, shape, kind in outs],
        in_specs=[pl.BlockSpec(memory_space=SPACES[kind]) for kind in kinds],
        out_specs=[pl.BlockSpec(memory_space=SPACES[space]) for space, _, _ in outs],
        scratch_shapes=list(scratch),
        compiler_params=pltpu.CompilerParams(vmem_limit_bytes=limit),
        cost_estimate=pl.CostEstimate(flops=flops, bytes_accessed=moved, transcendentals=0),
    )(*args)


def body(
    vectors,
    leaf_basis,
    transfer,
    sibling_coupling,
    list_coupling,
    near_tiles,
    tile_target,
    tile_source,
    tile_count,
    couple_offset,
    couple_class,
):
    columns, width = vectors.shape
    boxes, rank, points = leaf_basis.shape
    count = lax.axis_size(AXES)
    bits = count.bit_length() - 1
    steps = boxes.bit_length() - 1
    double = 2 * rank
    dma = pltpu.SemaphoreType.DMA

    def send(x, target):
        return lax.ppermute(x, AXES, [(i, target(i)) for i in range(count)])

    def turned(i, low, wide, step):
        digit = (i >> low) % 2**wide
        return i + (((digit + step) % 2**wide - digit) << low)

    before = send(vectors, lambda i: (i + 1) % count)
    ints = jnp.int32
    plain = (transfer, vectors, sibling_coupling)
    path_shapes = [(2 ** (height - 1), 2, rank, double) for height in range(1, steps + 1)]
    transfer, own, sibling, coeffs, leaf, *paths = call(
        leaf_kernel,
        "leaf",
        "hhhh",
        (*plain, leaf_basis),
        (
            *(("v", x.shape, x.dtype) for x in plain),
            ("v", (1, columns, double), BF16),
            ("v", (boxes, columns, rank), F32),
            *(("v", shape, F32) for shape in path_shapes),
        ),
        scratch=(pltpu.VMEM(leaf_basis.shape, BF16), dma((5,))),
    )
    device = lax.axis_index(AXES).astype(ints).reshape(1)
    window, passed = call(
        window_kernel,
        "window",
        "vvv",
        (coeffs, before, own),
        (("v", (2 * boxes, columns, points), BF16), ("v", coeffs.shape, BF16)),
    )
    lists = (tile_target, tile_source, couple_offset, couple_class)
    links = couple_offset.shape[1]
    gathered = coeffs
    after = send(own, lambda i: (i - 1) % count)
    for index, (low, wide) in enumerate(rounds_of(bits - 1)):
        kept = passed if index == 0 else gathered
        if index == 1:
            maps, rest, places, codes, kept, spread, local, targets, sources = call(
                functools.partial(map_kernel, bits),
                "maps",
                "shhhhhvvvv" + "v" * steps,
                (device, *lists, list_coupling, gathered, transfer, sibling, leaf, *paths),
                (
                    ("v", (count // 2 * double, double), BF16),
                    ("v", ((1 + links) * double, double), BF16),
                    ("v", (links, 8, 128), ints),
                    ("v", (links, columns, double), ints),
                    ("v", gathered.shape, BF16),
                    ("v", (2 * boxes * rank, 2 * double), BF16),
                    ("v", (columns, boxes * rank), F32),
                    ("v", tile_target.shape, ints),
                    ("v", tile_source.shape, ints),
                ),
                scratch=(
                    pltpu.SMEM(couple_offset.shape, ints),
                    pltpu.SMEM(couple_class.shape, ints),
                    pltpu.VMEM(list_coupling.shape, F32),
                    dma((5,)),
                ),
            )
        parts = [kept]
        for step in range(1, 2**wide):
            parts.append(send(gathered, lambda i, args=(low + 1, wide, step): turned(i, *args)))
        gathered = jnp.concatenate(parts, axis=0)
    blocks, total = call(
        functools.partial(half_kernel, bits),
        "half",
        "svv",
        (device, gathered, maps),
        (("v", (3, columns, double), BF16), ("v", (columns, double), F32)),
    )
    other = send(blocks, lambda i: i ^ 1)
    near, picked = call(
        near_kernel,
        "near",
        "sssvvvvvv",
        (tile_count, targets, sources, window, after, near_tiles, blocks, gathered, places),
        (("v", (boxes, columns, points), F32), ("v", (links, columns, double), BF16)),
        scratch=(pltpu.VMEM((boxes, columns, points), BF16),),
    )
    (field,) = call(
        field_kernel,
        "field",
        "v" * 9,
        (other, picked, codes, rest, total, spread, local, leaf_basis, near),
        (("v", (columns, width), F32),),
    )
    return field


def solution(mesh):
    in_specs = (
        P(None, AXES),
        P(AXES, None, None),
        P(),
        P(),
        P(),
        P(AXES, None, None),
        P(AXES),
        P(AXES),
        P(AXES),
        P(AXES, None),
        P(AXES, None),
    )
    return jax.shard_map(body, mesh=mesh, in_specs=in_specs, out_specs=P(None, AXES), check_vma=False)
```
